32 devices in a mesh: grp: 2 (over x), tok: 8 (over z, y), sub: 2 (over core).
Axes of the slice: x: 2, y: 2, z: 4, core: 2. Of those that a mesh axis runs over, the one named last changes fastest.
Arguments:
- patches: bfloat16 [4096, 1408], P(('grp', 'tok')), may hold values from -6 to 6
- image_sizes: int32 [16, 4], P(('grp', 'tok')), may hold values from 1 to 32, 64 in all within a row
- vision_inproj: bfloat16 [1408, 2, 3, 704], P('tok', 'sub'), may hold values from -0.15625 to 0.15625
- vision_outproj: bfloat16 [1408, 1408], P('sub', 'tok'), may hold values from -0.625 to 0.625
- merger_weight: bfloat16 [5632, 1408], P('tok', 'sub'), may hold values from -0.078125 to 0.078125
- text_embed: bfloat16 [2048, 1408], P(('grp', 'tok')), may hold values from -6 to 6
- image_positions: int32 [2, 512], P('grp', 'tok'), may hold values from 0 to 1023, as said below
- prompt_lengths: int32 [2, 2], P('grp'), may hold values from 1 to 896, 1024 in all within a row
- decoder_inproj: bfloat16 [1408, 2, 3, 704], P(('grp', 'tok'), 'sub'), may hold values from -0.15625 to 0.15625
- decoder_outproj: bfloat16 [1408, 1408], P('sub', ('grp', 'tok')), may hold values from -0.625 to 0.625
Outputs:
- text_update: bfloat16 [2048, 1408], P(('grp', 'tok', 'sub'))
The draws below stay inside these ranges and needn't reach their ends.
Inputs may be any that keep to these rules, and one draw needn't show every extreme that they name: `image_positions`: within each half the positions are distinct. Of the 64 merged tokens of one piece, at most 16 go to positions of any one block of 128 positions, and some reach that number. `image_sizes`: each row sums to 64. `prompt_lengths`: each row sums to 1024.
All inputs are finite; a program needn't handle non-finite values.
Results may differ from the reference program's by a relative error of at most 0.03.
Values may be sent and summed in bfloat16 or wider, within the bound.
A program may use at most 128 MiB of HBM per device.

```python
import math
import jax
import jax.numpy as jnp
import numpy as np
from jax import lax

HEADS = 16
HD = 88
D = 1408
VP = 256
PIECE = 128
IMGS = 4
REACH = 3
PROMPTS = 2
HALVES = 2
CHIPS = 16
PATCHES = 4096
G = 64
CAP = 16
TEXT_TOK = 2048
MAXLEN = 896
N_TOK = 8
N_SUB = 2


def draw_image_positions(key, part):

    def one_half(half_key):
        split_keys = jax.random.split(half_key, 3)
        is_hot = (jax.random.permutation(split_keys[0], N_TOK) < N_TOK // 4).astype(jnp.int32)
        priority = jax.random.randint(split_keys[1], (N_TOK, N_TOK), 0, 1024) + is_hot[None, :] * 768
        scores = priority * N_TOK + jnp.arange(N_TOK, dtype=jnp.int32)[None, :]
        unused, chosen = lax.top_k(scores, N_TOK // 2)
        chosen = jnp.sort(chosen.astype(jnp.int32), axis=1)
        source = jnp.arange(N_TOK, dtype=jnp.int32)[:, None]
        member = jnp.zeros((N_TOK, N_TOK), jnp.int32).at[source, chosen].set(1)
        before = jnp.cumsum(member, axis=0) - member
        piece_load = jnp.sum(member, axis=0) * CAP
        offset = jax.random.randint(split_keys[2], (N_TOK,), 0, PIECE - piece_load + 1)
        token_index = jnp.arange(G, dtype=jnp.int32)
        target = chosen[:, token_index // CAP]
        position = target * PIECE + offset[target] + before[source, target] * CAP + token_index[None, :] % CAP
        return position.reshape(N_TOK * G).astype(jnp.int32)
    return jax.vmap(one_half)(jax.random.split(key, HALVES))


def block_scale(stream_key, shape, cuts, smallest, high):
    def one(dim, shards_of):
        steps = jax.random.uniform(jax.random.fold_in(jax.random.fold_in(stream_key, 6), dim), (shards_of,), jnp.float32, smallest / len(cuts), high / len(cuts))
        return jnp.repeat(jnp.exp(steps), shape[dim] // shards_of).reshape((-1,) + (1,) * (len(shape) - dim - 1))

    gain = one(*cuts[0])
    for cut in cuts[1:]:
        gain = gain * one(*cut)
    return gain


def length_profile(count, total, limit, slope):
    loads = [(1 << 20) // math.isqrt(rank ** slope) + 1 for rank in range(2, count + 1)]
    spare, counts = total - limit - (count - 1), [1] * (count - 1)
    while spare > 0:
        movable = [i for i in range(count - 1) if counts[i] < limit]
        whole, budget = sum([loads[i] for i in movable]), spare
        for i in movable:
            extra = min(limit - counts[i], max(1, budget * loads[i] // whole), spare)
            counts[i] = counts[i] + extra
            spare = spare - extra
    return np.array([limit] + counts)


def ragged(rng, amount, total, limit, skew):
    if amount == 2:
        one = jax.random.randint(rng, (), max(1, total - limit), min(limit, total - 1) + 1)
        return jnp.stack([one, total - one])
    tallies = jnp.asarray(length_profile(amount, total, limit, skew), jnp.int32)
    couples = (amount - 1) // 2
    giver, taker = tallies[1:1 + 2 * couples:2], tallies[2:2 + 2 * couples:2]
    margin = jnp.minimum(giver - 1, limit - taker)
    shifted = jax.random.randint(jax.random.fold_in(rng, 1), (couples,), 0, 1 << 20) % (margin + 1)
    tallies = tallies.at[1:1 + 2 * couples:2].set(giver - shifted).at[2:2 + 2 * couples:2].set(taker + shifted)
    return tallies[jax.random.permutation(jax.random.fold_in(rng, 2), amount)]


def bell_draw(stream_key, extent, scale, bound, shards=(), held_as=jnp.bfloat16):
    factor_of = block_scale(stream_key, extent, shards, -0.22, 0.18) if shards else 1.0
    result = jax.random.normal(stream_key, extent, jnp.float32) * scale * factor_of
    return jnp.minimum(jnp.maximum(result, -bound), bound).astype(held_as)


def setup_inputs(seed: int = 0) -> dict:
    arg_keys = jax.random.split(jax.random.key(seed), 11)
    return {
        "patches": bell_draw(arg_keys[0], (PATCHES, D), 1.0, 6.0, ((0, 16),)),
        "image_sizes": jax.vmap(lambda own: ragged(own, IMGS, G, G // 2, 2))(jax.random.split(arg_keys[1], CHIPS)).reshape((CHIPS, IMGS)).astype(jnp.int32),
        "vision_inproj": bell_draw(arg_keys[2], (D, N_SUB, 3, D // N_SUB), D ** -0.5, 0.15625, ((0, 8), (1, 2))),
        "vision_outproj": bell_draw(arg_keys[3], (D, D), HD ** -0.5, 0.625, ((0, 2), (1, 8))),
        "merger_weight": bell_draw(arg_keys[4], (4 * D, D), (4 * D) ** -0.5, 0.078125, ((0, 8), (1, 2))),
        "text_embed": bell_draw(arg_keys[5], (TEXT_TOK, D), 1.0, 6.0, ((0, 16),)),
        "image_positions": draw_image_positions(jax.random.fold_in(arg_keys[10], 71), 0),
        "prompt_lengths": jax.vmap(lambda own: ragged(own, PROMPTS, N_TOK * PIECE, MAXLEN, 2))(jax.random.split(arg_keys[7], HALVES)).reshape((HALVES, PROMPTS)).astype(jnp.int32),
        "decoder_inproj": bell_draw(arg_keys[8], (D, N_SUB, 3, D // N_SUB), D ** -0.5, 0.15625, ((0, 16), (1, 2))),
        "decoder_outproj": bell_draw(arg_keys[9], (D, D), HD ** -0.5, 0.625, ((0, 2), (1, 16))),
    }


norm_eps = 1e-06

def layer_norm(values):
    center = values - lax.optimization_barrier(jnp.mean(values, axis=-1, keepdims=True))
    spread = lax.optimization_barrier(jnp.mean(center * center, axis=-1, keepdims=True))
    return center * lax.rsqrt(spread + norm_eps)

def attend(queries, keys_all, values_all, allowed):
    scores = jnp.einsum('qhe,khe->hqk', queries.astype(jnp.float32), keys_all.astype(jnp.float32)) * (1.0 / math.sqrt(HD))
    weights_raw = jnp.exp(scores) * allowed[None]
    weights = (weights_raw / lax.optimization_barrier(jnp.sum(weights_raw, axis=-1, keepdims=True))).astype(jnp.bfloat16)
    mixture = jnp.einsum('hqk,khe->qhe', weights.astype(jnp.float32), values_all.astype(jnp.float32))
    return mixture.astype(jnp.bfloat16).reshape(queries.shape[0], D)

def split_heads(projected, row_total):
    triple = projected.astype(jnp.bfloat16).reshape(row_total, N_SUB, 3, D // N_SUB)
    return [triple[:, :, member].reshape(row_total, HEADS, HD) for member in range(3)]

def reference(patches, image_sizes, vision_inproj, vision_outproj, merger_weight, text_embed, image_positions, prompt_lengths, decoder_inproj, decoder_outproj):

    def vision_chip(chip_args):
        chip_patches, chip_sizes = chip_args
        patch_rows = chip_patches.astype(jnp.float32)
        normed = layer_norm(patch_rows).astype(jnp.bfloat16)
        projected = jnp.dot(normed, vision_inproj.reshape(D, 3 * D), preferred_element_type=jnp.float32)
        queries, keys_all, values_all = split_heads(projected, VP)
        image_ends = jnp.cumsum(chip_sizes)
        group_ids = jnp.arange(VP, dtype=jnp.int32) // 4
        image_ids = lax.optimization_barrier(jnp.sum((group_ids[:, None] >= image_ends[None, :]).astype(jnp.int32), axis=1))
        same_image = (image_ids[:, None] == image_ids[None, :]).astype(jnp.float32)
        heads_out = attend(queries, keys_all, values_all, same_image)
        hidden = patch_rows + jnp.dot(heads_out, vision_outproj, preferred_element_type=jnp.float32)
        merged = layer_norm(hidden).astype(jnp.bfloat16).reshape(VP // 4, 4 * D)
        return jnp.dot(merged, merger_weight, preferred_element_type=jnp.float32).astype(jnp.bfloat16)
    images = lax.map(vision_chip, (patches.reshape(CHIPS, VP, D), image_sizes))
    half_rows = N_TOK * PIECE
    window_rows = (REACH + 1) * PIECE
    outputs = []
    for half_index in range(HALVES):
        text_rows = text_embed[half_index * half_rows:(half_index + 1) * half_rows]
        half_images = images[half_index * N_TOK:(half_index + 1) * N_TOK].reshape(N_TOK * (VP // 4), D)
        decoder_input = text_rows.at[image_positions[half_index]].set(half_images)
        normed = layer_norm(decoder_input.astype(jnp.float32)).astype(jnp.bfloat16)
        projected = jnp.dot(normed, decoder_inproj.reshape(D, 3 * D), preferred_element_type=jnp.float32)
        queries, keys_all, values_all = split_heads(projected, half_rows)
        front = jnp.zeros((REACH * PIECE, HEADS, HD), jnp.bfloat16)
        padded_keys = jnp.concatenate([front, keys_all], axis=0)
        padded_values = jnp.concatenate([front, values_all], axis=0)
        lengths = prompt_lengths[half_index]
        starts = jnp.cumsum(lengths) - lengths

        def one_piece(piece_index):
            query_pos = piece_index * PIECE + jnp.arange(PIECE, dtype=jnp.int32)
            key_pos = (piece_index - REACH) * PIECE + jnp.arange(window_rows, dtype=jnp.int32)
            query_start = lax.optimization_barrier(jnp.max(jnp.where(starts[None, :] <= query_pos[:, None], starts[None, :], 0), axis=1))
            allowed = ((key_pos[None, :] <= query_pos[:, None]) & (key_pos[None, :] >= query_start[:, None])).astype(jnp.float32)
            piece_queries = lax.dynamic_slice_in_dim(queries, piece_index * PIECE, PIECE, 0)
            piece_keys = lax.dynamic_slice_in_dim(padded_keys, piece_index * PIECE, window_rows, 0)
            piece_values = lax.dynamic_slice_in_dim(padded_values, piece_index * PIECE, window_rows, 0)
            return attend(piece_queries, piece_keys, piece_values, allowed)
        heads_out = lax.map(one_piece, jnp.arange(N_TOK, dtype=jnp.int32)).reshape(half_rows, D)
        outputs.append(jnp.dot(heads_out, decoder_outproj, preferred_element_type=jnp.float32).astype(jnp.bfloat16))
    return jnp.concatenate(outputs, axis=0)
```

```python
import functools
import math

import jax
import jax.numpy as jnp
from jax import lax
from jax.experimental import pallas as pl
from jax.experimental.pallas import tpu as pltpu
from jax.sharding import PartitionSpec as P

HD = 88
REACH = 3


norm_eps = 1e-06


def passed_along(block, axis, distance):
    devices = range(lax.axis_size(axis))
    route = [(i - distance, i) for i in devices if i - distance in devices]
    return lax.ppermute(block, axis, route)


def layer_norm(values):
    center = values - jnp.mean(values, axis=-1, keepdims=True)
    spread = jnp.mean(center * center, axis=-1, keepdims=True)
    return center * lax.rsqrt(spread + norm_eps)


def softmax_heads(queries, keys_all, values_all, allowed):
    scores = jnp.einsum("qhe,khe->hqk", queries, keys_all, preferred_element_type=jnp.float32) * (
        1.0 / math.sqrt(HD)
    )
    weights_raw = jnp.exp(scores) * allowed[None]
    weights = (weights_raw / jnp.sum(weights_raw, axis=-1, keepdims=True)).astype(jnp.bfloat16)
    mixture = jnp.einsum("hqk,khe->qhe", weights, values_all, preferred_element_type=jnp.float32)
    return mixture.astype(jnp.bfloat16)


def attend_blocks(queries, keys_all, values_all, allowed):
    row_total, head_count, head_size = queries.shape
    block_rows = min(row_total, 512)
    block_count = row_total // block_rows
    query_blocks = queries.reshape(block_count, block_rows, head_count, head_size)
    allow_blocks = allowed.reshape(block_count, block_rows, allowed.shape[1])
    outputs = lax.map(
        lambda block_pair: softmax_heads(block_pair[0], keys_all, values_all, block_pair[1]),
        (query_blocks, allow_blocks),
    )
    return outputs.reshape(row_total, head_count * head_size)


def shards_general(
    patches,
    image_sizes,
    vision_inproj,
    vision_outproj,
    merger_weight,
    text_embed,
    image_positions,
    prompt_lengths,
    decoder_inproj,
    decoder_outproj,
):
    inproj_full, outproj_full, merger_full = (
        lax.all_gather(vision_inproj, "tok", axis=0, tiled=True),
        lax.all_gather(vision_outproj, "tok", axis=1, tiled=True),
        lax.all_gather(merger_weight, "tok", axis=0, tiled=True),
    )
    patch_count, width = patches.shape
    half_width = inproj_full.shape[3]
    head_local = half_width // HD
    patch_rows = patches.astype(jnp.float32)
    normed = layer_norm(patch_rows).astype(jnp.bfloat16)
    projected = jnp.dot(
        normed, inproj_full.reshape(width, 3 * half_width), preferred_element_type=jnp.float32
    )
    triple = projected.astype(jnp.bfloat16).reshape(patch_count, 3, head_local, HD)
    image_ends = jnp.cumsum(image_sizes[0])
    group_ids = jnp.arange(patch_count, dtype=jnp.int32) // 4
    image_ids = jnp.sum((group_ids[:, None] >= image_ends[None, :]).astype(jnp.int32), axis=1)
    same_image = (image_ids[:, None] == image_ids[None, :]).astype(jnp.float32)
    heads_out = attend_blocks(triple[:, 0], triple[:, 1], triple[:, 2], same_image)
    partial_value = jnp.dot(heads_out, outproj_full, preferred_element_type=jnp.float32)
    hidden = patch_rows + lax.psum(partial_value.astype(jnp.bfloat16), "sub").astype(jnp.float32)
    merged = layer_norm(hidden).astype(jnp.bfloat16).reshape(patch_count // 4, 4 * width)
    piece_count = lax.axis_size("tok")
    capacity = patch_count // (2 * piece_count)
    piece_rows = text_embed.shape[0]
    targets = image_positions[0]
    target_chip = targets // piece_rows
    target_row = targets % piece_rows
    chip_hits = (target_chip[:, None] == jnp.arange(piece_count, dtype=jnp.int32)[None, :]).astype(
        jnp.int32
    )
    slot_index = jnp.sum((jnp.cumsum(chip_hits, axis=0) - chip_hits) * chip_hits, axis=1)
    row_buffer = (
        jnp.full((piece_count, capacity), piece_rows, jnp.int32)
        .at[target_chip, slot_index]
        .set(target_row)
    )
    embedded = jnp.dot(merged, merger_full, preferred_element_type=jnp.float32).astype(jnp.bfloat16)
    narrow_rows = lax.all_to_all(
        jnp.zeros((piece_count, capacity, embedded.shape[1]), embedded.dtype)
        .at[target_chip, slot_index]
        .set(embedded),
        "tok",
        split_axis=0,
        concat_axis=0,
        tiled=True,
    )
    arrived_rows = lax.all_to_all(row_buffer, "tok", split_axis=0, concat_axis=0, tiled=True)
    image_half = narrow_rows.reshape(piece_count * capacity, half_width)
    image_full = lax.all_gather(image_half, "sub", axis=1, tiled=True)
    decoder_input = text_embed.at[arrived_rows.reshape(-1)].set(image_full, mode="drop")
    text_inproj, text_outproj = (
        lax.all_gather(decoder_inproj, ("grp", "tok"), axis=0, tiled=True),
        lax.all_gather(decoder_outproj, ("grp", "tok"), axis=1, tiled=True),
    )
    normed_text = layer_norm(decoder_input.astype(jnp.float32)).astype(jnp.bfloat16)
    text_proj = jnp.dot(
        normed_text, text_inproj.reshape(width, 3 * half_width), preferred_element_type=jnp.float32
    )
    text_triple = text_proj.astype(jnp.bfloat16).reshape(piece_rows, 3, head_local, HD)
    own_pair = text_triple[:, 1:].reshape(piece_rows, 2 * half_width)
    earlier = [own_pair]
    carried = own_pair
    for step_back in range(REACH):
        carried = passed_along(carried, "tok", 1)
        earlier.append(carried)
    window = jnp.concatenate(earlier[::-1], axis=0).reshape(
        (REACH + 1) * piece_rows, 2, head_local, HD
    )
    piece_id = lax.axis_index("tok")
    query_pos = piece_id * piece_rows + jnp.arange(piece_rows, dtype=jnp.int32)
    key_pos = (piece_id - REACH) * piece_rows + jnp.arange(
        (REACH + 1) * piece_rows, dtype=jnp.int32
    )
    lengths = prompt_lengths[0]
    starts = jnp.cumsum(lengths) - lengths
    query_start = jnp.max(
        jnp.where(starts[None, :] <= query_pos[:, None], starts[None, :], 0), axis=1
    )
    allowed = (
        (key_pos[None, :] <= query_pos[:, None]) & (key_pos[None, :] >= query_start[:, None])
    ).astype(jnp.float32)
    text_heads = attend_blocks(text_triple[:, 0], window[:, 0], window[:, 1], allowed)
    text_partial = jnp.dot(text_heads, text_outproj, preferred_element_type=jnp.float32)
    return lax.psum_scatter(
        text_partial.astype(jnp.bfloat16), "sub", scatter_dimension=0, tiled=True
    )


LANES = 128
MESH = pl.DeviceIdType.MESH


def head_kernel(
    kind, n_tok, x_ref, w_ref, info_ref, out_ref, buf, staged, kv, send_sem, recv_sem, back_send, back_recv
):
    me, core = lax.axis_index("tok"), lax.axis_index("sub")
    rows = 2 * x_ref.shape[0]
    z, y = lax.div(me, 2), lax.rem(me, 2)
    n_z = n_tok // 2
    side = me + 1 - 2 * y

    barrier = pltpu.get_barrier_semaphore()
    for d in range(1, n_tok):
        pl.semaphore_signal(
            barrier, inc=1, device_id={"tok": lax.rem(me + d, n_tok)}, device_id_type=MESH
        )
    pl.semaphore_signal(barrier, inc=1, device_id={"sub": 1 - core}, device_id_type=MESH)

    own = x_ref[...].astype(jnp.float32)
    buf[me, core] = layer_norm(own).astype(jnp.bfloat16)
    pl.semaphore_wait(barrier, n_tok)

    def push(t, way):
        target = [{"tok": me + 2}, {"tok": me - 2}, {"tok": side}, {"sub": 1 - core}][way]
        return pltpu.make_async_remote_copy(
            src_ref=buf.at[t, core],
            dst_ref=buf.at[t, core],
            send_sem=send_sem.at[way, t],
            recv_sem=recv_sem.at[t, core],
            device_id=target,
            device_id_type=MESH,
        )

    def arrived(t, c):
        pltpu.make_async_remote_copy(
            src_ref=buf.at[t, c],
            dst_ref=buf.at[t, c],
            send_sem=send_sem.at[3, t],
            recv_sem=recv_sem.at[t, c],
            device_id={"sub": 1 - core},
            device_id_type=MESH,
        ).wait_recv()

    def run(act, wait):
        @pl.when(z < n_z - 1)
        def _():
            act(me, 0)

        @pl.when(z > 0)
        def _():
            act(me, 1)

        act(me, 2)
        act(me, 3)
        for k in range(1, n_z + 1):
            if k < n_z:
                @pl.when(z - k >= 0)
                def _():
                    wait(me - 2 * k)

                    @pl.when(z < n_z - 1)
                    def _():
                        act(me - 2 * k, 0)

                    act(me - 2 * k, 2)
                    act(me - 2 * k, 3)

                @pl.when(z + k < n_z)
                def _():
                    wait(me + 2 * k)

                    @pl.when(z > 0)
                    def _():
                        act(me + 2 * k, 1)

                    act(me + 2 * k, 2)
                    act(me + 2 * k, 3)
            if k == 1:
                wait(side)
                act(side, 3)
            else:
                @pl.when(z - k + 1 >= 0)
                def _():
                    wait(side - 2 * k + 2)
                    act(side - 2 * k + 2, 3)

                @pl.when(z + k - 1 < n_z)
                def _():
                    wait(side + 2 * k - 2)
                    act(side + 2 * k - 2, 3)

    run(lambda t, way: push(t, way).start(), lambda t: arrived(t, core))
    for t in range(n_tok):
        arrived(t, 1 - core)

    def project(j):
        block = buf[j].reshape(rows, buf.shape[3])
        return jnp.dot(block, w_ref[...], preferred_element_type=jnp.float32).astype(jnp.bfloat16)

    def mix(query, key, value, allowed):
        scores = lax.dot_general(
            query, key, (((1,), (1,)), ((), ())), preferred_element_type=jnp.float32
        ) * (1.0 / math.sqrt(HD))
        raw = jnp.where(allowed, jnp.exp(scores), 0.0)
        weights = (raw / jnp.sum(raw, axis=-1, keepdims=True)).astype(jnp.bfloat16)
        return jnp.dot(weights, value, preferred_element_type=jnp.float32).astype(jnp.bfloat16)

    def back(j):
        return pltpu.make_async_remote_copy(
            src_ref=staged.at[j],
            dst_ref=out_ref.at[me],
            send_sem=back_send.at[j],
            recv_sem=back_recv.at[me],
            device_id={"tok": j},
            device_id_type=MESH,
        )

    if kind == "text":
        kv[pl.ds(0, REACH)] = jnp.zeros((REACH, rows, 3 * LANES), jnp.bfloat16)

        def fill(j, carry):
            kv[j + REACH] = project(j)
            return carry

        lax.fori_loop(0, n_tok, fill, 0)

    def piece(d, carry):
        j = lax.rem(me + d, n_tok)
        if kind == "image":
            proj = project(j)
            query, key, value = (proj[:, i * LANES : (i + 1) * LANES] for i in range(3))
            left = lax.div(lax.broadcasted_iota(jnp.int32, (rows, 1), 0), 4)
            right = lax.div(lax.broadcasted_iota(jnp.int32, (1, rows), 1), 4)
            left_id, right_id = jnp.zeros_like(left), jnp.zeros_like(right)
            for i in range(info_ref.shape[1]):
                end = info_ref[j, i]
                left_id = left_id + jnp.where(left >= end, 1, 0)
                right_id = right_id + jnp.where(right >= end, 1, 0)
            allowed = left_id == right_id
        else:
            span = (REACH + 1) * rows
            query = kv[j + REACH, :, 0:LANES]
            key = kv[pl.ds(j, REACH + 1), :, LANES : 2 * LANES].reshape(span, LANES)
            value = kv[pl.ds(j, REACH + 1), :, 2 * LANES : 3 * LANES].reshape(span, LANES)
            query_pos = j * rows + lax.broadcasted_iota(jnp.int32, (rows, 1), 0)
            key_pos = (j - REACH) * rows + lax.broadcasted_iota(jnp.int32, (1, span), 1)
            begin = jnp.zeros_like(query_pos)
            for i in range(info_ref.shape[1]):
                first = info_ref[0, i]
                begin = jnp.maximum(begin, jnp.where(query_pos >= first, first, 0))
            allowed = (key_pos <= query_pos) & (key_pos >= begin)
        mixture = mix(query, key, value, allowed)

        @pl.when(d < n_tok)
        def _():
            staged[j] = mixture
            back(j).start()

        @pl.when(d == n_tok)
        def _():
            out_ref[me] = mixture

        return carry

    lax.fori_loop(1, n_tok + 1, piece, 0)

    run(lambda t, way: push(t, way).wait_send(), lambda t: None)
    for d in range(1, n_tok):
        j = lax.rem(me + d, n_tok)
        back(j).wait_send()
        pltpu.make_async_remote_copy(
            src_ref=staged.at[j],
            dst_ref=out_ref.at[j],
            send_sem=back_send.at[j],
            recv_sem=back_recv.at[j],
            device_id={"tok": j},
            device_id_type=MESH,
        ).wait_recv()


def heads_of(kind, half_rows, weight, info, n_tok):
    half, width = half_rows.shape
    rows = 2 * half
    kv_shape = (n_tok + REACH, rows, 3 * LANES) if kind == "text" else (1, 16, LANES)
    vmem = pl.BlockSpec(memory_space=pltpu.VMEM)
    total = n_tok * rows
    return pl.pallas_call(
        functools.partial(head_kernel, kind, n_tok),
        out_shape=jax.ShapeDtypeStruct((n_tok, rows, LANES), jnp.bfloat16),
        in_specs=[vmem, vmem, pl.BlockSpec(memory_space=pltpu.SMEM)],
        out_specs=vmem,
        scratch_shapes=[
            pltpu.VMEM((n_tok, 2, half, width), jnp.bfloat16),
            pltpu.VMEM((n_tok, rows, LANES), jnp.bfloat16),
            pltpu.VMEM(kv_shape, jnp.bfloat16),
            pltpu.SemaphoreType.DMA((4, n_tok)),
            pltpu.SemaphoreType.DMA((n_tok, 2)),
            pltpu.SemaphoreType.DMA((n_tok,)),
            pltpu.SemaphoreType.DMA((n_tok,)),
        ],
        compiler_params=pltpu.CompilerParams(
            collective_id=0 if kind == "image" else 1,
            has_side_effects=True,
            vmem_limit_bytes=40 * 1024 * 1024,
        ),
        cost_estimate=pl.CostEstimate(
            flops=2 * total * width * 3 * LANES, bytes_accessed=2 * total * width, transcendentals=0
        ),
    )(half_rows, weight, info)


def head_columns(weight, head_local):
    rows = weight.shape[0]
    split = weight.reshape(rows, 3, head_local, HD).transpose(2, 0, 1, 3)
    split = jnp.pad(split, ((0, 0), (0, 0), (0, 0), (0, LANES - HD)))
    return split.reshape(head_local, rows, 3 * LANES)


def head_rows(weight, head_local):
    split = weight.reshape(head_local, HD, weight.shape[1])
    return jnp.pad(split, ((0, 0), (0, LANES - HD), (0, 0)))


def across(block, axis):
    return lax.all_to_all(block, axis, split_axis=0, concat_axis=0, tiled=True)


def shards(
    patches,
    image_sizes,
    vision_inproj,
    vision_outproj,
    merger_weight,
    text_embed,
    image_positions,
    prompt_lengths,
    decoder_inproj,
    decoder_outproj,
):
    n_tok = lax.axis_size("tok")
    half_width = vision_inproj.shape[3]
    head_local = half_width // HD
    if n_tok != head_local or lax.axis_size("sub") != 2:
        return shards_general(
            patches,
            image_sizes,
            vision_inproj,
            vision_outproj,
            merger_weight,
            text_embed,
            image_positions,
            prompt_lengths,
            decoder_inproj,
            decoder_outproj,
        )
    core = lax.axis_index("sub")
    patch_count, width = patches.shape
    piece_rows = text_embed.shape[0]
    bf16, f32 = jnp.bfloat16, jnp.float32

    vision_weight = across(head_columns(vision_inproj, head_local), "tok").reshape(width, 3 * LANES)
    text_part = across(head_columns(decoder_inproj, head_local), "tok").reshape(-1, 3 * LANES)
    text_weight = lax.all_gather(text_part, "grp", axis=0, tiled=True)
    vision_out = head_rows(lax.all_gather(vision_outproj, "tok", axis=1, tiled=True), head_local)
    text_out = head_rows(
        lax.all_gather(decoder_outproj, ("grp", "tok"), axis=1, tiled=True), head_local
    )

    image_ends = lax.all_gather(jnp.cumsum(image_sizes, axis=1), "tok", axis=0, tiled=True)
    half_patches = lax.dynamic_slice_in_dim(patches, core * (patch_count // 2), patch_count // 2, 0)
    heads = heads_of("image", half_patches, vision_weight, image_ends, n_tok)
    partial_value = jnp.einsum("hrc,hcn->rn", heads, vision_out, preferred_element_type=f32).astype(
        bf16
    )
    other = lax.ppermute(partial_value, "sub", [(0, 1), (1, 0)])
    hidden = patches.astype(f32) + (partial_value.astype(f32) + other.astype(f32))
    merged = layer_norm(hidden).astype(bf16)

    group_count = patch_count // 4
    shard_depth = merger_weight.shape[0]
    parts = 4 * width // shard_depth
    cut = merged.reshape(group_count, 4, parts // 4, shard_depth).transpose(1, 2, 0, 3)
    gathered = across(cut.reshape(parts, group_count, shard_depth), "tok")
    partial_embed = jnp.dot(
        gathered.reshape(n_tok * group_count, shard_depth), merger_weight, preferred_element_type=f32
    ).astype(bf16)
    embedded = jnp.sum(
        across(partial_embed.reshape(n_tok, group_count, half_width), "tok").astype(f32), axis=0
    ).astype(bf16)

    capacity = patch_count // (2 * n_tok)
    targets = image_positions[0]
    target_chip = targets // piece_rows
    target_row = targets % piece_rows
    chip_hits = (target_chip[:, None] == jnp.arange(n_tok, dtype=jnp.int32)[None, :]).astype(jnp.int32)
    slot_index = jnp.sum((jnp.cumsum(chip_hits, axis=0) - chip_hits) * chip_hits, axis=1)
    slot = target_chip * capacity + slot_index
    slot_hit = jnp.arange(n_tok * capacity, dtype=jnp.int32)[:, None] == slot[None, :]
    row_buffer = jnp.sum(jnp.where(slot_hit, target_row[None, :] + 1, 0), axis=1) - 1
    arrived_rows = across(row_buffer.reshape(n_tok, capacity), "tok").reshape(-1)
    packed = jnp.dot(slot_hit.astype(bf16), embedded, preferred_element_type=f32).astype(bf16)
    narrow_rows = across(packed.reshape(n_tok, capacity, half_width), "tok").reshape(-1, half_width)
    row_hit = jnp.arange(piece_rows, dtype=jnp.int32)[:, None] == arrived_rows[None, :]
    placed = jnp.dot(row_hit.astype(bf16), narrow_rows, preferred_element_type=f32).astype(bf16)
    half_piece = piece_rows // 2
    swapped = across(placed.reshape(2, half_piece, half_width), "sub")
    image_rows = swapped.transpose(1, 0, 2).reshape(half_piece, width)
    filled = lax.dynamic_slice_in_dim(
        jnp.any(row_hit, axis=1).astype(jnp.int32), core * half_piece, half_piece, 0
    )
    text_half = lax.dynamic_slice_in_dim(text_embed, core * half_piece, half_piece, 0)
    decoder_input = jnp.where(filled[:, None] > 0, image_rows, text_half)

    starts = jnp.cumsum(prompt_lengths, axis=1) - prompt_lengths
    text_heads = heads_of("text", decoder_input, text_weight, starts, n_tok)
    text_partial = jnp.einsum("hrc,hcn->rn", text_heads, text_out, preferred_element_type=f32)
    pair = across(text_partial.astype(bf16).reshape(2, half_piece, width), "sub")
    return jnp.sum(pair.astype(f32), axis=0).astype(bf16)


def solution(mesh):
    placed = (
        P(("grp", "tok"), None),
        P(("grp", "tok"), None),
        P("tok", "sub", None, None),
        P("sub", "tok"),
        P("tok", "sub"),
        P(("grp", "tok"), None),
        P("grp", "tok"),
        P("grp", None),
        P(("grp", "tok"), "sub", None, None),
        P("sub", ("grp", "tok")),
    )
    return jax.shard_map(
        shards,
        mesh=mesh,
        in_specs=placed,
        out_specs=P(("grp", "tok", "sub"), None),
        check_vma=False,
    )
```

```python
import functools
import math

import jax
import jax.numpy as jnp
from jax import lax
from jax.experimental import pallas as pl
from jax.experimental.pallas import tpu as pltpu
from jax.sharding import PartitionSpec as P

HD = 88
REACH = 3


norm_eps = 1e-06


def passed_along(block, axis, distance):
    devices = range(lax.axis_size(axis))
    route = [(i - distance, i) for i in devices if i - distance in devices]
    return lax.ppermute(block, axis, route)


def layer_norm(values):
    center = values - jnp.mean(values, axis=-1, keepdims=True)
    spread = jnp.mean(center * center, axis=-1, keepdims=True)
    return center * lax.rsqrt(spread + norm_eps)


def softmax_heads(queries, keys_all, values_all, allowed):
    scores = jnp.einsum("qhe,khe->hqk", queries, keys_all, preferred_element_type=jnp.float32) * (
        1.0 / math.sqrt(HD)
    )
    weights_raw = jnp.exp(scores) * allowed[None]
    weights = (weights_raw / jnp.sum(weights_raw, axis=-1, keepdims=True)).astype(jnp.bfloat16)
    mixture = jnp.einsum("hqk,khe->qhe", weights, values_all, preferred_element_type=jnp.float32)
    return mixture.astype(jnp.bfloat16)


def attend_blocks(queries, keys_all, values_all, allowed):
    row_total, head_count, head_size = queries.shape
    block_rows = min(row_total, 512)
    block_count = row_total // block_rows
    query_blocks = queries.reshape(block_count, block_rows, head_count, head_size)
    allow_blocks = allowed.reshape(block_count, block_rows, allowed.shape[1])
    outputs = lax.map(
        lambda block_pair: softmax_heads(block_pair[0], keys_all, values_all, block_pair[1]),
        (query_blocks, allow_blocks),
    )
    return outputs.reshape(row_total, head_count * head_size)


def shards_general(
    patches,
    image_sizes,
    vision_inproj,
    vision_outproj,
    merger_weight,
    text_embed,
    image_positions,
    prompt_lengths,
    decoder_inproj,
    decoder_outproj,
):
    inproj_full, outproj_full, merger_full = (
        lax.all_gather(vision_inproj, "tok", axis=0, tiled=True),
        lax.all_gather(vision_outproj, "tok", axis=1, tiled=True),
        lax.all_gather(merger_weight, "tok", axis=0, tiled=True),
    )
    patch_count, width = patches.shape
    half_width = inproj_full.shape[3]
    head_local = half_width // HD
    patch_rows = patches.astype(jnp.float32)
    normed = layer_norm(patch_rows).astype(jnp.bfloat16)
    projected = jnp.dot(
        normed, inproj_full.reshape(width, 3 * half_width), preferred_element_type=jnp.float32
    )
    triple = projected.astype(jnp.bfloat16).reshape(patch_count, 3, head_local, HD)
    image_ends = jnp.cumsum(image_sizes[0])
    group_ids = jnp.arange(patch_count, dtype=jnp.int32) // 4
    image_ids = jnp.sum((group_ids[:, None] >= image_ends[None, :]).astype(jnp.int32), axis=1)
    same_image = (image_ids[:, None] == image_ids[None, :]).astype(jnp.float32)
    heads_out = attend_blocks(triple[:, 0], triple[:, 1], triple[:, 2], same_image)
    partial_value = jnp.dot(heads_out, outproj_full, preferred_element_type=jnp.float32)
    hidden = patch_rows + lax.psum(partial_value.astype(jnp.bfloat16), "sub").astype(jnp.float32)
    merged = layer_norm(hidden).astype(jnp.bfloat16).reshape(patch_count // 4, 4 * width)
    piece_count = lax.axis_size("tok")
    capacity = patch_count // (2 * piece_count)
    piece_rows = text_embed.shape[0]
    targets = image_positions[0]
    target_chip = targets // piece_rows
    target_row = targets % piece_rows
    chip_hits = (target_chip[:, None] == jnp.arange(piece_count, dtype=jnp.int32)[None, :]).astype(
        jnp.int32
    )
    slot_index = jnp.sum((jnp.cumsum(chip_hits, axis=0) - chip_hits) * chip_hits, axis=1)
    row_buffer = (
        jnp.full((piece_count, capacity), piece_rows, jnp.int32)
        .at[target_chip, slot_index]
        .set(target_row)
    )
    embedded = jnp.dot(merged, merger_full, preferred_element_type=jnp.float32).astype(jnp.bfloat16)
    narrow_rows = lax.all_to_all(
        jnp.zeros((piece_count, capacity, embedded.shape[1]), embedded.dtype)
        .at[target_chip, slot_index]
        .set(embedded),
        "tok",
        split_axis=0,
        concat_axis=0,
        tiled=True,
    )
    arrived_rows = lax.all_to_all(row_buffer, "tok", split_axis=0, concat_axis=0, tiled=True)
    image_half = narrow_rows.reshape(piece_count * capacity, half_width)
    image_full = lax.all_gather(image_half, "sub", axis=1, tiled=True)
    decoder_input = text_embed.at[arrived_rows.reshape(-1)].set(image_full, mode="drop")
    text_inproj, text_outproj = (
        lax.all_gather(decoder_inproj, ("grp", "tok"), axis=0, tiled=True),
        lax.all_gather(decoder_outproj, ("grp", "tok"), axis=1, tiled=True),
    )
    normed_text = layer_norm(decoder_input.astype(jnp.float32)).astype(jnp.bfloat16)
    text_proj = jnp.dot(
        normed_text, text_inproj.reshape(width, 3 * half_width), preferred_element_type=jnp.float32
    )
    text_triple = text_proj.astype(jnp.bfloat16).reshape(piece_rows, 3, head_local, HD)
    own_pair = text_triple[:, 1:].reshape(piece_rows, 2 * half_width)
    earlier = [own_pair]
    carried = own_pair
    for step_back in range(REACH):
        carried = passed_along(carried, "tok", 1)
        earlier.append(carried)
    window = jnp.concatenate(earlier[::-1], axis=0).reshape(
        (REACH + 1) * piece_rows, 2, head_local, HD
    )
    piece_id = lax.axis_index("tok")
    query_pos = piece_id * piece_rows + jnp.arange(piece_rows, dtype=jnp.int32)
    key_pos = (piece_id - REACH) * piece_rows + jnp.arange(
        (REACH + 1) * piece_rows, dtype=jnp.int32
    )
    lengths = prompt_lengths[0]
    starts = jnp.cumsum(lengths) - lengths
    query_start = jnp.max(
        jnp.where(starts[None, :] <= query_pos[:, None], starts[None, :], 0), axis=1
    )
    allowed = (
        (key_pos[None, :] <= query_pos[:, None]) & (key_pos[None, :] >= query_start[:, None])
    ).astype(jnp.float32)
    text_heads = attend_blocks(text_triple[:, 0], window[:, 0], window[:, 1], allowed)
    text_partial = jnp.dot(text_heads, text_outproj, preferred_element_type=jnp.float32)
    return lax.psum_scatter(
        text_partial.astype(jnp.bfloat16), "sub", scatter_dimension=0, tiled=True
    )


LANES = 128
MESH = pl.DeviceIdType.MESH


def head_kernel(
    kind, n_tok, x_ref, w_ref, info_ref, out_ref, buf, staged, kv, send_sem, recv_sem, back_send, back_recv
):
    me, core = lax.axis_index("tok"), lax.axis_index("sub")
    rows = 2 * x_ref.shape[0]
    z, y = lax.div(me, 2), lax.rem(me, 2)
    n_z = n_tok // 2
    side = me + 1 - 2 * y

    barrier = pltpu.get_barrier_semaphore()
    for d in range(1, n_tok):
        pl.semaphore_signal(
            barrier, inc=1, device_id={"tok": lax.rem(me + d, n_tok)}, device_id_type=MESH
        )
    pl.semaphore_signal(barrier, inc=1, device_id={"sub": 1 - core}, device_id_type=MESH)

    own = x_ref[...].astype(jnp.float32)
    buf[me, core] = layer_norm(own).astype(jnp.bfloat16)
    pl.semaphore_wait(barrier, n_tok)

    def push(t, way):
        target = [{"tok": me + 2}, {"tok": me - 2}, {"tok": side}, {"sub": 1 - core}][way]
        return pltpu.make_async_remote_copy(
            src_ref=buf.at[t, core],
            dst_ref=buf.at[t, core],
            send_sem=send_sem.at[way, t],
            recv_sem=recv_sem.at[t, core],
            device_id=target,
            device_id_type=MESH,
        )

    def arrived(t, c):
        pltpu.make_async_remote_copy(
            src_ref=buf.at[t, c],
            dst_ref=buf.at[t, c],
            send_sem=send_sem.at[3, t],
            recv_sem=recv_sem.at[t, c],
            device_id={"sub": 1 - core},
            device_id_type=MESH,
        ).wait_recv()

    def run(act, wait):
        @pl.when(z < n_z - 1)
        def _():
            act(me, 0)

        @pl.when(z > 0)
        def _():
            act(me, 1)

        act(me, 2)
        act(me, 3)
        for k in range(1, n_z + 1):
            if k < n_z:
                @pl.when(z - k >= 0)
                def _():
                    wait(me - 2 * k)

                    @pl.when(z < n_z - 1)
                    def _():
                        act(me - 2 * k, 0)

                    act(me - 2 * k, 2)
                    act(me - 2 * k, 3)

                @pl.when(z + k < n_z)
                def _():
                    wait(me + 2 * k)

                    @pl.when(z > 0)
                    def _():
                        act(me + 2 * k, 1)

                    act(me + 2 * k, 2)
                    act(me + 2 * k, 3)
            if k == 1:
                wait(side)
                act(side, 3)
            else:
                @pl.when(z - k + 1 >= 0)
                def _():
                    wait(side - 2 * k + 2)
                    act(side - 2 * k + 2, 3)

                @pl.when(z + k - 1 < n_z)
                def _():
                    wait(side + 2 * k - 2)
                    act(side + 2 * k - 2, 3)

    run(lambda t, way: push(t, way).start(), lambda t: arrived(t, core))
    for t in range(n_tok):
        arrived(t, 1 - core)

    def project(j):
        block = buf[j].reshape(rows, buf.shape[3])
        return jnp.dot(block, w_ref[...], preferred_element_type=jnp.float32).astype(jnp.bfloat16)

    def mix(query, key, value, allowed):
        scores = lax.dot_general(
            query, key, (((1,), (1,)), ((), ())), preferred_element_type=jnp.float32
        ) * (1.0 / math.sqrt(HD))
        raw = jnp.where(allowed, jnp.exp(scores), 0.0)
        weights = (raw / jnp.sum(raw, axis=-1, keepdims=True)).astype(jnp.bfloat16)
        return jnp.dot(weights, value, preferred_element_type=jnp.float32).astype(jnp.bfloat16)

    def back(j):
        return pltpu.make_async_remote_copy(
            src_ref=staged.at[j],
            dst_ref=out_ref.at[me],
            send_sem=back_send.at[j],
            recv_sem=back_recv.at[me],
            device_id={"tok": j},
            device_id_type=MESH,
        )

    if kind == "text":
        kv[pl.ds(0, REACH)] = jnp.zeros((REACH, rows, 3 * LANES), jnp.bfloat16)

        def fill(j, carry):
            kv[j + REACH] = project(j)
            return carry

        lax.fori_loop(0, n_tok, fill, 0)

    def piece(d, carry):
        j = lax.rem(me + d, n_tok)
        if kind == "image":
            proj = project(j)
            query, key, value = (proj[:, i * LANES : (i + 1) * LANES] for i in range(3))
            left = lax.div(lax.broadcasted_iota(jnp.int32, (rows, 1), 0), 4)
            right = lax.div(lax.broadcasted_iota(jnp.int32, (1, rows), 1), 4)
            left_id, right_id = jnp.zeros_like(left), jnp.zeros_like(right)
            for i in range(info_ref.shape[1]):
                end = info_ref[j, i]
                left_id = left_id + jnp.where(left >= end, 1, 0)
                right_id = right_id + jnp.where(right >= end, 1, 0)
            allowed = left_id == right_id
        else:
            span = (REACH + 1) * rows
            query = kv[j + REACH, :, 0:LANES]
            key = kv[pl.ds(j, REACH + 1), :, LANES : 2 * LANES].reshape(span, LANES)
            value = kv[pl.ds(j, REACH + 1), :, 2 * LANES : 3 * LANES].reshape(span, LANES)
            query_pos = j * rows + lax.broadcasted_iota(jnp.int32, (rows, 1), 0)
            key_pos = (j - REACH) * rows + lax.broadcasted_iota(jnp.int32, (1, span), 1)
            begin = jnp.zeros_like(query_pos)
            for i in range(info_ref.shape[1]):
                first = info_ref[0, i]
                begin = jnp.maximum(begin, jnp.where(query_pos >= first, first, 0))
            allowed = (key_pos <= query_pos) & (key_pos >= begin)
        mixture = mix(query, key, value, allowed)

        @pl.when(d < n_tok)
        def _():
            staged[j] = mixture
            back(j).start()

        @pl.when(d == n_tok)
        def _():
            out_ref[me] = mixture

        return carry

    lax.fori_loop(1, n_tok + 1, piece, 0)

    run(lambda t, way: push(t, way).wait_send(), lambda t: None)
    for d in range(1, n_tok):
        j = lax.rem(me + d, n_tok)
        back(j).wait_send()
        pltpu.make_async_remote_copy(
            src_ref=staged.at[j],
            dst_ref=out_ref.at[j],
            send_sem=back_send.at[j],
            recv_sem=back_recv.at[j],
            device_id={"tok": j},
            device_id_type=MESH,
        ).wait_recv()


def merge_kernel(
    n_tok,
    heads_ref,
    out_weight_ref,
    patches_ref,
    merger_ref,
    slot_hit_ref,
    row_hit_ref,
    out_ref,
    give,
    got,
    cut,
    gathered,
    totals,
    parts,
    packed,
    arrived,
    placed,
    pair_sem,
    cut_send,
    cut_recv,
    core_send,
    core_recv,
    part_send,
    part_recv,
    pack_send,
    pack_recv,
):
    me, core = lax.axis_index("tok"), lax.axis_index("sub")
    half, width = give.shape
    quarter = half // 4
    depth = merger_ref.shape[0]

    barrier = pltpu.get_barrier_semaphore()
    for d in range(1, n_tok):
        pl.semaphore_signal(
            barrier, inc=1, device_id={"tok": lax.rem(me + d, n_tok)}, device_id_type=MESH
        )
    pl.semaphore_signal(barrier, inc=1, device_id={"sub": 1 - core}, device_id_type=MESH)

    def send(src, dst, send_sem, recv_sem, target):
        return pltpu.make_async_remote_copy(
            src_ref=src,
            dst_ref=dst,
            send_sem=send_sem,
            recv_sem=recv_sem,
            device_id=target,
            device_id_type=MESH,
        )

    def projected(c):
        total = jnp.zeros((half, width), jnp.float32)
        for h in range(n_tok):
            total = total + jnp.dot(
                heads_ref[h, pl.ds(pl.multiple_of(c * half, half), half)],
                out_weight_ref[h],
                preferred_element_type=jnp.float32,
            )
        return total.astype(jnp.bfloat16)

    sibling = {"sub": 1 - core}
    give[...] = projected(1 - core)
    pl.semaphore_wait(barrier, n_tok)
    swap = send(give, got, pair_sem.at[0], pair_sem.at[1], sibling)
    swap.start()
    kept = projected(core)
    swap.wait()
    rows = patches_ref[pl.ds(pl.multiple_of(core * half, half), half)].astype(jnp.float32)
    hidden = rows + (kept.astype(jnp.float32) + got[...].astype(jnp.float32))
    merged = layer_norm(hidden).astype(jnp.bfloat16)
    to_row = lax.broadcasted_iota(jnp.int32, (half, half), 0)
    from_row = lax.broadcasted_iota(jnp.int32, (half, half), 1)
    pick = jnp.where(
        from_row == 4 * lax.rem(to_row, quarter) + lax.div(to_row, quarter), 1.0, 0.0
    ).astype(jnp.bfloat16)
    split = jnp.dot(pick, merged, preferred_element_type=jnp.float32).astype(jnp.bfloat16)
    per_row = width // depth
    for t in range(n_tok):
        j, u = t // per_row, t % per_row
        cut[t] = split[j * quarter : (j + 1) * quarter, u * depth : (u + 1) * depth]

    def cut_copy(t, source):
        return send(
            cut.at[t], gathered.at[source, core], cut_send.at[t], cut_recv.at[source], {"tok": t}
        )

    def core_copy(t, c):
        return send(
            gathered.at[t, c], gathered.at[t, c], core_send.at[t], core_recv.at[t], sibling
        )

    def part_copy(t, source):
        return send(totals.at[t], parts.at[source], part_send.at[t], part_recv.at[source], {"tok": t})

    def pack_copy(t, source):
        return send(packed.at[t], arrived.at[source], pack_send.at[t], pack_recv.at[source], {"tok": t})

    others = [lax.rem(me + d, n_tok) for d in range(1, n_tok)]
    backward = [lax.rem(me + n_tok - d, n_tok) for d in range(1, n_tok)]
    for t in others:
        cut_copy(t, me).start()
    gathered[me, core] = cut[me]
    core_copy(me, core).start()
    for t in backward:
        cut_copy(t, t).wait_recv()
        core_copy(t, core).start()

    def meet(t):
        core_copy(t, 1 - core).wait_recv()
        block = gathered[t].reshape(2 * quarter, depth)
        return jnp.dot(block, merger_ref[...], preferred_element_type=jnp.float32).astype(jnp.bfloat16)

    parts[me] = meet(me)
    for t in backward:
        totals[t] = meet(t)
        part_copy(t, me).start()
    total = parts[me].astype(jnp.float32)
    for t in others:
        part_copy(t, t).wait_recv()
        total = total + parts[t].astype(jnp.float32)
    sums = total.astype(jnp.bfloat16)
    capacity = packed.shape[1]
    slots = jnp.dot(slot_hit_ref[...], sums, preferred_element_type=jnp.float32).astype(jnp.bfloat16)
    packed[...] = slots.reshape(n_tok, capacity, slots.shape[1])
    for t in others:
        pack_copy(t, me).start()
    arrived[me] = packed[me]
    for t in backward:
        pack_copy(t, t).wait_recv()
    tokens = arrived[...].reshape(n_tok * capacity, arrived.shape[2])
    landed = jnp.dot(row_hit_ref[...], tokens, preferred_element_type=jnp.float32).astype(jnp.bfloat16)
    placed[...] = landed.reshape(placed.shape)
    last = send(placed.at[1 - core], out_ref.at[core], pair_sem.at[2], pair_sem.at[3], sibling)
    last.start()
    out_ref[core] = placed[core]
    last.wait()
    core_copy(me, core).wait_send()
    for t in others:
        cut_copy(t, me).wait_send()
        core_copy(t, core).wait_send()
        part_copy(t, me).wait_send()
        pack_copy(t, me).wait_send()


def merged_tokens(heads, out_weight, patches, merger_weight, slot_hit, row_hit, n_tok):
    count, width = patches.shape
    depth, narrow = merger_weight.shape
    groups, capacity = count // 4, slot_hit.shape[0] // n_tok
    piece_rows = row_hit.shape[0]
    bf16 = jnp.bfloat16
    vmem = pl.BlockSpec(memory_space=pltpu.VMEM)
    each = pltpu.SemaphoreType.DMA((n_tok,))
    return pl.pallas_call(
        functools.partial(merge_kernel, n_tok),
        out_shape=jax.ShapeDtypeStruct((2, piece_rows // 2, narrow), bf16),
        in_specs=[vmem] * 6,
        out_specs=vmem,
        scratch_shapes=[
            pltpu.VMEM((count // 2, width), bf16),
            pltpu.VMEM((count // 2, width), bf16),
            pltpu.VMEM((n_tok, groups // 2, depth), bf16),
            pltpu.VMEM((n_tok, 2, groups // 2, depth), bf16),
            pltpu.VMEM((n_tok, groups, narrow), bf16),
            pltpu.VMEM((n_tok, groups, narrow), bf16),
            pltpu.VMEM((n_tok, capacity, narrow), bf16),
            pltpu.VMEM((n_tok, capacity, narrow), bf16),
            pltpu.VMEM((2, piece_rows // 2, narrow), bf16),
            pltpu.SemaphoreType.DMA((4,)),
        ]
        + [each] * 8,
        compiler_params=pltpu.CompilerParams(
            collective_id=2, has_side_effects=True, vmem_limit_bytes=40 * 1024 * 1024
        ),
        cost_estimate=pl.CostEstimate(
            flops=2 * count * width * n_tok * LANES, bytes_accessed=8 * count * width, transcendentals=0
        ),
    )(heads, out_weight, patches, merger_weight, slot_hit, row_hit)


def heads_of(kind, half_rows, weight, info, n_tok):
    half, width = half_rows.shape
    rows = 2 * half
    kv_shape = (n_tok + REACH, rows, 3 * LANES) if kind == "text" else (1, 16, LANES)
    vmem = pl.BlockSpec(memory_space=pltpu.VMEM)
    total = n_tok * rows
    return pl.pallas_call(
        functools.partial(head_kernel, kind, n_tok),
        out_shape=jax.ShapeDtypeStruct((n_tok, rows, LANES), jnp.bfloat16),
        in_specs=[vmem, vmem, pl.BlockSpec(memory_space=pltpu.SMEM)],
        out_specs=vmem,
        scratch_shapes=[
            pltpu.VMEM((n_tok, 2, half, width), jnp.bfloat16),
            pltpu.VMEM((n_tok, rows, LANES), jnp.bfloat16),
            pltpu.VMEM(kv_shape, jnp.bfloat16),
            pltpu.SemaphoreType.DMA((4, n_tok)),
            pltpu.SemaphoreType.DMA((n_tok, 2)),
            pltpu.SemaphoreType.DMA((n_tok,)),
            pltpu.SemaphoreType.DMA((n_tok,)),
        ],
        compiler_params=pltpu.CompilerParams(
            collective_id=0 if kind == "image" else 1,
            has_side_effects=True,
            vmem_limit_bytes=40 * 1024 * 1024,
        ),
        cost_estimate=pl.CostEstimate(
            flops=2 * total * width * 3 * LANES, bytes_accessed=2 * total * width, transcendentals=0
        ),
    )(half_rows, weight, info)


def head_columns(weight, head_local):
    rows = weight.shape[0]
    split = weight.reshape(rows, 3, head_local, HD).transpose(2, 0, 1, 3)
    split = jnp.pad(split, ((0, 0), (0, 0), (0, 0), (0, LANES - HD)))
    return split.reshape(head_local, rows, 3 * LANES)


def head_rows(weight, head_local):
    split = weight.reshape(head_local, HD, weight.shape[1])
    return jnp.pad(split, ((0, 0), (0, LANES - HD), (0, 0)))


def across(block, axis):
    return lax.all_to_all(block, axis, split_axis=0, concat_axis=0, tiled=True)


def shards(
    patches,
    image_sizes,
    vision_inproj,
    vision_outproj,
    merger_weight,
    text_embed,
    image_positions,
    prompt_lengths,
    decoder_inproj,
    decoder_outproj,
):
    n_tok = lax.axis_size("tok")
    half_width = vision_inproj.shape[3]
    head_local = half_width // HD
    if n_tok != head_local or lax.axis_size("sub") != 2:
        return shards_general(
            patches,
            image_sizes,
            vision_inproj,
            vision_outproj,
            merger_weight,
            text_embed,
            image_positions,
            prompt_lengths,
            decoder_inproj,
            decoder_outproj,
        )
    core = lax.axis_index("sub")
    patch_count, width = patches.shape
    piece_rows = text_embed.shape[0]
    bf16, f32 = jnp.bfloat16, jnp.float32

    vision_weight = across(head_columns(vision_inproj, head_local), "tok").reshape(width, 3 * LANES)
    text_part = across(head_columns(decoder_inproj, head_local), "tok").reshape(-1, 3 * LANES)
    text_weight = lax.all_gather(text_part, "grp", axis=0, tiled=True)
    vision_out = head_rows(lax.all_gather(vision_outproj, "tok", axis=1, tiled=True), head_local)
    text_out = head_rows(
        lax.all_gather(decoder_outproj, ("grp", "tok"), axis=1, tiled=True), head_local
    )

    capacity = patch_count // (2 * n_tok)
    targets = image_positions[0]
    target_chip = targets // piece_rows
    target_row = targets % piece_rows
    chip_hits = (target_chip[:, None] == jnp.arange(n_tok, dtype=jnp.int32)[None, :]).astype(jnp.int32)
    slot_index = jnp.sum((jnp.cumsum(chip_hits, axis=0) - chip_hits) * chip_hits, axis=1)
    slot = target_chip * capacity + slot_index
    slot_hit = jnp.arange(n_tok * capacity, dtype=jnp.int32)[:, None] == slot[None, :]
    row_buffer = jnp.sum(jnp.where(slot_hit, target_row[None, :] + 1, 0), axis=1) - 1
    own_ends = jnp.broadcast_to(jnp.cumsum(image_sizes, axis=1), (n_tok, image_sizes.shape[1]))
    numbers = across(
        jnp.concatenate([row_buffer.reshape(n_tok, capacity), own_ends], axis=1), "tok"
    )
    arrived_rows, image_ends = numbers[:, :capacity].reshape(-1), numbers[:, capacity:]
    row_hit = jnp.arange(piece_rows, dtype=jnp.int32)[:, None] == arrived_rows[None, :]

    half_patches = lax.dynamic_slice_in_dim(patches, core * (patch_count // 2), patch_count // 2, 0)
    heads = heads_of("image", half_patches, vision_weight, image_ends, n_tok)
    halves = merged_tokens(
        heads, vision_out, patches, merger_weight, slot_hit.astype(bf16), row_hit.astype(bf16), n_tok
    )
    half_piece = piece_rows // 2
    image_rows = halves.transpose(1, 0, 2).reshape(half_piece, width)
    filled = lax.dynamic_slice_in_dim(
        jnp.any(row_hit, axis=1).astype(jnp.int32), core * half_piece, half_piece, 0
    )
    text_half = lax.dynamic_slice_in_dim(text_embed, core * half_piece, half_piece, 0)
    decoder_input = jnp.where(filled[:, None] > 0, image_rows, text_half)

    starts = jnp.cumsum(prompt_lengths, axis=1) - prompt_lengths
    text_heads = heads_of("text", decoder_input, text_weight, starts, n_tok)
    text_partial = jnp.einsum("hrc,hcn->rn", text_heads, text_out, preferred_element_type=f32)
    pair = across(text_partial.astype(bf16).reshape(2, half_piece, width), "sub")
    return jnp.sum(pair.astype(f32), axis=0).astype(bf16)


def solution(mesh):
    placed = (
        P(("grp", "tok"), None),
        P(("grp", "tok"), None),
        P("tok", "sub", None, None),
        P("sub", "tok"),
        P("tok", "sub"),
        P(("grp", "tok"), None),
        P("grp", "tok"),
        P("grp", None),
        P(("grp", "tok"), "sub", None, None),
        P("sub", ("grp", "tok")),
    )
    return jax.shard_map(
        shards,
        mesh=mesh,
        in_specs=placed,
        out_specs=P(("grp", "tok", "sub"), None),
        check_vma=False,
    )
```

```python
import functools
import math

import jax
import jax.numpy as jnp
from jax import lax
from jax.experimental import pallas as pl
from jax.experimental.pallas import tpu as pltpu
from jax.sharding import PartitionSpec as P

HD = 88
REACH = 3


norm_eps = 1e-06


def passed_along(block, axis, distance):
    devices = range(lax.axis_size(axis))
    route = [(i - distance, i) for i in devices if i - distance in devices]
    return lax.ppermute(block, axis, route)


def layer_norm(values):
    center = values - jnp.mean(values, axis=-1, keepdims=True)
    spread = jnp.mean(center * center, axis=-1, keepdims=True)
    return center * lax.rsqrt(spread + norm_eps)


def softmax_heads(queries, keys_all, values_all, allowed):
    scores = jnp.einsum("qhe,khe->hqk", queries, keys_all, preferred_element_type=jnp.float32) * (
        1.0 / math.sqrt(HD)
    )
    weights_raw = jnp.exp(scores) * allowed[None]
    weights = (weights_raw / jnp.sum(weights_raw, axis=-1, keepdims=True)).astype(jnp.bfloat16)
    mixture = jnp.einsum("hqk,khe->qhe", weights, values_all, preferred_element_type=jnp.float32)
    return mixture.astype(jnp.bfloat16)


def attend_blocks(queries, keys_all, values_all, allowed):
    row_total, head_count, head_size = queries.shape
    block_rows = min(row_total, 512)
    block_count = row_total // block_rows
    query_blocks = queries.reshape(block_count, block_rows, head_count, head_size)
    allow_blocks = allowed.reshape(block_count, block_rows, allowed.shape[1])
    outputs = lax.map(
        lambda block_pair: softmax_heads(block_pair[0], keys_all, values_all, block_pair[1]),
        (query_blocks, allow_blocks),
    )
    return outputs.reshape(row_total, head_count * head_size)


def shards_general(
    patches,
    image_sizes,
    vision_inproj,
    vision_outproj,
    merger_weight,
    text_embed,
    image_positions,
    prompt_lengths,
    decoder_inproj,
    decoder_outproj,
):
    inproj_full, outproj_full, merger_full = (
        lax.all_gather(vision_inproj, "tok", axis=0, tiled=True),
        lax.all_gather(vision_outproj, "tok", axis=1, tiled=True),
        lax.all_gather(merger_weight, "tok", axis=0, tiled=True),
    )
    patch_count, width = patches.shape
    half_width = inproj_full.shape[3]
    head_local = half_width // HD
    patch_rows = patches.astype(jnp.float32)
    normed = layer_norm(patch_rows).astype(jnp.bfloat16)
    projected = jnp.dot(
        normed, inproj_full.reshape(width, 3 * half_width), preferred_element_type=jnp.float32
    )
    triple = projected.astype(jnp.bfloat16).reshape(patch_count, 3, head_local, HD)
    image_ends = jnp.cumsum(image_sizes[0])
    group_ids = jnp.arange(patch_count, dtype=jnp.int32) // 4
    image_ids = jnp.sum((group_ids[:, None] >= image_ends[None, :]).astype(jnp.int32), axis=1)
    same_image = (image_ids[:, None] == image_ids[None, :]).astype(jnp.float32)
    heads_out = attend_blocks(triple[:, 0], triple[:, 1], triple[:, 2], same_image)
    partial_value = jnp.dot(heads_out, outproj_full, preferred_element_type=jnp.float32)
    hidden = patch_rows + lax.psum(partial_value.astype(jnp.bfloat16), "sub").astype(jnp.float32)
    merged = layer_norm(hidden).astype(jnp.bfloat16).reshape(patch_count // 4, 4 * width)
    piece_count = lax.axis_size("tok")
    capacity = patch_count // (2 * piece_count)
    piece_rows = text_embed.shape[0]
    targets = image_positions[0]
    target_chip = targets // piece_rows
    target_row = targets % piece_rows
    chip_hits = (target_chip[:, None] == jnp.arange(piece_count, dtype=jnp.int32)[None, :]).astype(
        jnp.int32
    )
    slot_index = jnp.sum((jnp.cumsum(chip_hits, axis=0) - chip_hits) * chip_hits, axis=1)
    row_buffer = (
        jnp.full((piece_count, capacity), piece_rows, jnp.int32)
        .at[target_chip, slot_index]
        .set(target_row)
    )
    embedded = jnp.dot(merged, merger_full, preferred_element_type=jnp.float32).astype(jnp.bfloat16)
    narrow_rows = lax.all_to_all(
        jnp.zeros((piece_count, capacity, embedded.shape[1]), embedded.dtype)
        .at[target_chip, slot_index]
        .set(embedded),
        "tok",
        split_axis=0,
        concat_axis=0,
        tiled=True,
    )
    arrived_rows = lax.all_to_all(row_buffer, "tok", split_axis=0, concat_axis=0, tiled=True)
    image_half = narrow_rows.reshape(piece_count * capacity, half_width)
    image_full = lax.all_gather(image_half, "sub", axis=1, tiled=True)
    decoder_input = text_embed.at[arrived_rows.reshape(-1)].set(image_full, mode="drop")
    text_inproj, text_outproj = (
        lax.all_gather(decoder_inproj, ("grp", "tok"), axis=0, tiled=True),
        lax.all_gather(decoder_outproj, ("grp", "tok"), axis=1, tiled=True),
    )
    normed_text = layer_norm(decoder_input.astype(jnp.float32)).astype(jnp.bfloat16)
    text_proj = jnp.dot(
        normed_text, text_inproj.reshape(width, 3 * half_width), preferred_element_type=jnp.float32
    )
    text_triple = text_proj.astype(jnp.bfloat16).reshape(piece_rows, 3, head_local, HD)
    own_pair = text_triple[:, 1:].reshape(piece_rows, 2 * half_width)
    earlier = [own_pair]
    carried = own_pair
    for step_back in range(REACH):
        carried = passed_along(carried, "tok", 1)
        earlier.append(carried)
    window = jnp.concatenate(earlier[::-1], axis=0).reshape(
        (REACH + 1) * piece_rows, 2, head_local, HD
    )
    piece_id = lax.axis_index("tok")
    query_pos = piece_id * piece_rows + jnp.arange(piece_rows, dtype=jnp.int32)
    key_pos = (piece_id - REACH) * piece_rows + jnp.arange(
        (REACH + 1) * piece_rows, dtype=jnp.int32
    )
    lengths = prompt_lengths[0]
    starts = jnp.cumsum(lengths) - lengths
    query_start = jnp.max(
        jnp.where(starts[None, :] <= query_pos[:, None], starts[None, :], 0), axis=1
    )
    allowed = (
        (key_pos[None, :] <= query_pos[:, None]) & (key_pos[None, :] >= query_start[:, None])
    ).astype(jnp.float32)
    text_heads = attend_blocks(text_triple[:, 0], window[:, 0], window[:, 1], allowed)
    text_partial = jnp.dot(text_heads, text_outproj, preferred_element_type=jnp.float32)
    return lax.psum_scatter(
        text_partial.astype(jnp.bfloat16), "sub", scatter_dimension=0, tiled=True
    )


LANES = 128
MESH = pl.DeviceIdType.MESH


def head_kernel(
    kind,
    n_tok,
    x_ref,
    weight_ref,
    info_ref,
    *rest,
):
    if kind == "image":
        out_ref, buf, staged, kv, send_sem, recv_sem, back_send, back_recv, *own_scratch = rest
        w_ref, w_send, w_recv, w_pass = own_scratch
        mixed = out_ref
    else:
        last_weight_ref, out_ref, buf, staged, kv, send_sem, recv_sem, back_send, back_recv, *own_scratch = rest
        mixed, give, got, pair_sem = own_scratch
        w_ref = weight_ref
    me, core, grp = lax.axis_index("tok"), lax.axis_index("sub"), lax.axis_index("grp")
    rows = 2 * x_ref.shape[0]
    z, y = lax.div(me, 2), lax.rem(me, 2)
    n_z = n_tok // 2
    side = me + 1 - 2 * y

    barrier = pltpu.get_barrier_semaphore()
    for d in range(1, n_tok):
        pl.semaphore_signal(
            barrier, inc=1, device_id={"tok": lax.rem(me + d, n_tok)}, device_id_type=MESH
        )
    pl.semaphore_signal(barrier, inc=1, device_id={"sub": 1 - core}, device_id_type=MESH)

    greeted = n_tok
    if kind == "image":
        pl.semaphore_signal(barrier, inc=1, device_id={"grp": 1 - grp}, device_id_type=MESH)
        greeted = n_tok + 1
        w_ref[me] = weight_ref[me]
    own = x_ref[...].astype(jnp.float32)
    buf[me, core] = layer_norm(own).astype(jnp.bfloat16)
    pl.semaphore_wait(barrier, greeted)

    def push(t, way):
        target = [{"tok": me + 2}, {"tok": me - 2}, {"tok": side}, {"sub": 1 - core}][way]
        return pltpu.make_async_remote_copy(
            src_ref=buf.at[t, core],
            dst_ref=buf.at[t, core],
            send_sem=send_sem.at[way, t],
            recv_sem=recv_sem.at[t, core],
            device_id=target,
            device_id_type=MESH,
        )

    def arrived(t, c):
        pltpu.make_async_remote_copy(
            src_ref=buf.at[t, c],
            dst_ref=buf.at[t, c],
            send_sem=send_sem.at[3, t],
            recv_sem=recv_sem.at[t, c],
            device_id={"sub": 1 - core},
            device_id_type=MESH,
        ).wait_recv()

    def run(act, wait):
        @pl.when(z < n_z - 1)
        def _():
            act(me, 0)

        @pl.when(z > 0)
        def _():
            act(me, 1)

        act(me, 2)
        act(me, 3)
        for k in range(1, n_z + 1):
            if k < n_z:
                @pl.when(z - k >= 0)
                def _():
                    wait(me - 2 * k)

                    @pl.when(z < n_z - 1)
                    def _():
                        act(me - 2 * k, 0)

                    act(me - 2 * k, 2)
                    act(me - 2 * k, 3)

                @pl.when(z + k < n_z)
                def _():
                    wait(me + 2 * k)

                    @pl.when(z > 0)
                    def _():
                        act(me + 2 * k, 1)

                    act(me + 2 * k, 2)
                    act(me + 2 * k, 3)
            if k == 1:
                wait(side)
                act(side, 3)
            else:
                @pl.when(z - k + 1 >= 0)
                def _():
                    wait(side - 2 * k + 2)
                    act(side - 2 * k + 2, 3)

                @pl.when(z + k - 1 < n_z)
                def _():
                    wait(side + 2 * k - 2)
                    act(side + 2 * k - 2, 3)

    def weight_copy(t, source):
        return pltpu.make_async_remote_copy(
            src_ref=weight_ref.at[t],
            dst_ref=w_ref.at[source],
            send_sem=w_send.at[t],
            recv_sem=w_recv.at[source],
            device_id={"tok": t},
            device_id_type=MESH,
        )

    def weight_pass(t):
        return pltpu.make_async_remote_copy(
            src_ref=w_ref.at[t],
            dst_ref=w_ref.at[t],
            send_sem=w_pass.at[t],
            recv_sem=w_recv.at[t],
            device_id={"grp": 1 - grp},
            device_id_type=MESH,
        )

    others = [lax.rem(me + d, n_tok) for d in range(1, n_tok)]

    def mine(t):
        return lax.rem(lax.div(t, 2), 2) == grp

    if kind == "image":
        @pl.when(mine(me))
        def _():
            for t in others:
                weight_copy(t, me).start()

    run(lambda t, way: push(t, way).start(), lambda t: arrived(t, core))
    if kind == "image":
        for t in others:
            @pl.when(mine(t))
            def _():
                weight_copy(t, t).wait_recv()
                weight_pass(t).start()

        for t in others:
            @pl.when(jnp.logical_not(mine(t)))
            def _():
                weight_pass(t).wait_recv()

    for t in range(n_tok):
        arrived(t, 1 - core)

    def project(j):
        block = buf[j].reshape(rows, buf.shape[3])
        weight = w_ref[...].reshape(buf.shape[3], 3 * LANES)
        return jnp.dot(block, weight, preferred_element_type=jnp.float32).astype(jnp.bfloat16)

    def mix(query, key, value, allowed):
        scores = lax.dot_general(
            query, key, (((1,), (1,)), ((), ())), preferred_element_type=jnp.float32
        ) * (1.0 / math.sqrt(HD))
        raw = jnp.where(allowed, jnp.exp(scores), 0.0)
        weights = (raw / jnp.sum(raw, axis=-1, keepdims=True)).astype(jnp.bfloat16)
        return jnp.dot(weights, value, preferred_element_type=jnp.float32).astype(jnp.bfloat16)

    def back(j):
        return pltpu.make_async_remote_copy(
            src_ref=staged.at[j],
            dst_ref=mixed.at[me],
            send_sem=back_send.at[j],
            recv_sem=back_recv.at[me],
            device_id={"tok": j},
            device_id_type=MESH,
        )

    if kind == "text":
        kv[pl.ds(0, REACH)] = jnp.zeros((REACH, rows, 3 * LANES), jnp.bfloat16)

        def fill(j, carry):
            kv[j + REACH] = project(j)
            return carry

        lax.fori_loop(0, n_tok, fill, 0)

    def piece(d, carry):
        j = lax.rem(me + d, n_tok)
        if kind == "image":
            proj = project(j)
            query, key, value = (proj[:, i * LANES : (i + 1) * LANES] for i in range(3))
            left = lax.div(lax.broadcasted_iota(jnp.int32, (rows, 1), 0), 4)
            right = lax.div(lax.broadcasted_iota(jnp.int32, (1, rows), 1), 4)
            left_id, right_id = jnp.zeros_like(left), jnp.zeros_like(right)
            for i in range(info_ref.shape[1]):
                end = info_ref[j, i]
                left_id = left_id + jnp.where(left >= end, 1, 0)
                right_id = right_id + jnp.where(right >= end, 1, 0)
            allowed = left_id == right_id
        else:
            span = (REACH + 1) * rows
            query = kv[j + REACH, :, 0:LANES]
            key = kv[pl.ds(j, REACH + 1), :, LANES : 2 * LANES].reshape(span, LANES)
            value = kv[pl.ds(j, REACH + 1), :, 2 * LANES : 3 * LANES].reshape(span, LANES)
            query_pos = j * rows + lax.broadcasted_iota(jnp.int32, (rows, 1), 0)
            key_pos = (j - REACH) * rows + lax.broadcasted_iota(jnp.int32, (1, span), 1)
            begin = jnp.zeros_like(query_pos)
            for i in range(info_ref.shape[1]):
                first = info_ref[0, i]
                begin = jnp.maximum(begin, jnp.where(query_pos >= first, first, 0))
            allowed = (key_pos <= query_pos) & (key_pos >= begin)
        mixture = mix(query, key, value, allowed)

        @pl.when(d < n_tok)
        def _():
            staged[j] = mixture
            back(j).start()

        @pl.when(d == n_tok)
        def _():
            mixed[me] = mixture

        return carry

    lax.fori_loop(1, n_tok + 1, piece, 0)

    run(lambda t, way: push(t, way).wait_send(), lambda t: None)
    for d in range(1, n_tok):
        j = lax.rem(me + d, n_tok)
        back(j).wait_send()
        pltpu.make_async_remote_copy(
            src_ref=staged.at[j],
            dst_ref=mixed.at[j],
            send_sem=back_send.at[j],
            recv_sem=back_recv.at[j],
            device_id={"tok": j},
            device_id_type=MESH,
        ).wait_recv()
    if kind == "image":
        @pl.when(mine(me))
        def _():
            for t in others:
                weight_copy(t, me).wait_send()

        for t in others:
            @pl.when(mine(t))
            def _():
                weight_pass(t).wait_send()

        return

    half = rows // 2

    def projected(c):
        total = jnp.zeros((half, out_ref.shape[1]), jnp.float32)
        for h in range(n_tok):
            total = total + lax.dot_general(
                mixed[h, pl.ds(pl.multiple_of(c * half, half), half)],
                last_weight_ref[:, h * LANES : (h + 1) * LANES],
                (((1,), (1,)), ((), ())),
                preferred_element_type=jnp.float32,
            )
        return total.astype(jnp.bfloat16)

    give[...] = projected(1 - core)
    swap = pltpu.make_async_remote_copy(
        src_ref=give,
        dst_ref=got,
        send_sem=pair_sem.at[0],
        recv_sem=pair_sem.at[1],
        device_id={"sub": 1 - core},
        device_id_type=MESH,
    )
    swap.start()
    kept = projected(core)
    swap.wait()
    out_ref[...] = (kept.astype(jnp.float32) + got[...].astype(jnp.float32)).astype(jnp.bfloat16)


def heads_of(kind, half_rows, weight, info, n_tok, last_weight=None):
    half, width = half_rows.shape
    rows = 2 * half
    bf16 = jnp.bfloat16
    vmem = pl.BlockSpec(memory_space=pltpu.VMEM)
    total = n_tok * rows
    each = pltpu.SemaphoreType.DMA((n_tok,))
    mixed = (n_tok, rows, LANES)
    operands = [half_rows, weight, info]
    if kind == "image":
        out_shape, kv_shape = mixed, (1, 16, LANES)
        extra = [pltpu.VMEM(weight.shape, bf16), each, each, each]
    else:
        out_shape, kv_shape = (half, width), (n_tok + REACH, rows, 3 * LANES)
        operands.append(last_weight)
        extra = [
            pltpu.VMEM(mixed, bf16),
            pltpu.VMEM((half, width), bf16),
            pltpu.VMEM((half, width), bf16),
            pltpu.SemaphoreType.DMA((2,)),
        ]
    return pl.pallas_call(
        functools.partial(head_kernel, kind, n_tok),
        out_shape=jax.ShapeDtypeStruct(out_shape, bf16),
        in_specs=[vmem, vmem, pl.BlockSpec(memory_space=pltpu.SMEM)] + [vmem] * (len(operands) - 3),
        out_specs=vmem,
        scratch_shapes=[
            pltpu.VMEM((n_tok, 2, half, width), bf16),
            pltpu.VMEM(mixed, bf16),
            pltpu.VMEM(kv_shape, bf16),
            pltpu.SemaphoreType.DMA((4, n_tok)),
            pltpu.SemaphoreType.DMA((n_tok, 2)),
            each,
            each,
        ]
        + extra,
        compiler_params=pltpu.CompilerParams(
            collective_id=0 if kind == "image" else 1,
            has_side_effects=True,
            vmem_limit_bytes=40 * 1024 * 1024,
        ),
        cost_estimate=pl.CostEstimate(
            flops=2 * total * width * 3 * LANES, bytes_accessed=2 * total * width, transcendentals=0
        ),
    )(*operands)


def head_columns(weight, head_local):
    rows = weight.shape[0]
    split = weight.reshape(rows, 3, head_local, HD).transpose(2, 0, 1, 3)
    split = jnp.pad(split, ((0, 0), (0, 0), (0, 0), (0, LANES - HD)))
    return split.reshape(head_local, rows, 3 * LANES)


def turned(weight, head_local):
    split = weight.T.reshape(weight.shape[1], head_local, HD)
    split = jnp.pad(split, ((0, 0), (0, 0), (0, LANES - HD)))
    return split.reshape(weight.shape[1], head_local * LANES)


def across(block, axis):
    return lax.all_to_all(block, axis, split_axis=0, concat_axis=0, tiled=True)


def merge_kernel(
    n_tok,
    heads_ref,
    out_weight_ref,
    patches_ref,
    merger_ref,
    slot_hit_ref,
    row_hit_ref,
    text_weight_ref,
    out_ref,
    text_out_ref,
    give,
    got,
    cut,
    gathered,
    totals,
    parts,
    packed,
    arrived,
    placed,
    pair_sem,
    cut_send,
    cut_recv,
    core_send,
    core_recv,
    part_send,
    part_recv,
    pack_send,
    pack_recv,
    text_send,
    text_recv,
    text_pass,
):
    me, core, grp = lax.axis_index("tok"), lax.axis_index("sub"), lax.axis_index("grp")
    half, width = give.shape
    quarter = half // 4
    depth = merger_ref.shape[0]

    barrier = pltpu.get_barrier_semaphore()
    for d in range(1, n_tok):
        pl.semaphore_signal(
            barrier, inc=1, device_id={"tok": lax.rem(me + d, n_tok)}, device_id_type=MESH
        )
    pl.semaphore_signal(barrier, inc=1, device_id={"sub": 1 - core}, device_id_type=MESH)
    pl.semaphore_signal(barrier, inc=1, device_id={"grp": 1 - grp}, device_id_type=MESH)

    def send(src, dst, send_sem, recv_sem, target):
        return pltpu.make_async_remote_copy(
            src_ref=src,
            dst_ref=dst,
            send_sem=send_sem,
            recv_sem=recv_sem,
            device_id=target,
            device_id_type=MESH,
        )

    def projected(c):
        total = jnp.zeros((half, width), jnp.float32)
        for h in range(n_tok):
            total = total + lax.dot_general(
                heads_ref[h, pl.ds(pl.multiple_of(c * half, half), half)],
                out_weight_ref[:, h * LANES : (h + 1) * LANES],
                (((1,), (1,)), ((), ())),
                preferred_element_type=jnp.float32,
            )
        return total.astype(jnp.bfloat16)

    sibling = {"sub": 1 - core}
    def text_copy(t, source):
        return send(
            text_weight_ref.at[t],
            text_out_ref.at[grp * n_tok + source],
            text_send.at[t],
            text_recv.at[grp * n_tok + source],
            {"tok": t},
        )

    def text_forward(t, g):
        slot = g * n_tok + t
        return send(
            text_out_ref.at[slot],
            text_out_ref.at[slot],
            text_pass.at[t],
            text_recv.at[slot],
            {"grp": 1 - grp},
        )

    others = [lax.rem(me + d, n_tok) for d in range(1, n_tok)]
    backward = [lax.rem(me + n_tok - d, n_tok) for d in range(1, n_tok)]
    text_out_ref[grp * n_tok + me] = text_weight_ref[me]
    pl.semaphore_wait(barrier, n_tok + 1)
    for t in others:
        text_copy(t, me).start()
    text_forward(me, grp).start()
    give[...] = projected(1 - core)
    swap = send(give, got, pair_sem.at[0], pair_sem.at[1], sibling)
    swap.start()
    kept = projected(core)
    swap.wait()
    rows = patches_ref[pl.ds(pl.multiple_of(core * half, half), half)].astype(jnp.float32)
    hidden = rows + (kept.astype(jnp.float32) + got[...].astype(jnp.float32))
    merged = layer_norm(hidden).astype(jnp.bfloat16)
    to_row = lax.broadcasted_iota(jnp.int32, (half, half), 0)
    from_row = lax.broadcasted_iota(jnp.int32, (half, half), 1)
    pick = jnp.where(
        from_row == 4 * lax.rem(to_row, quarter) + lax.div(to_row, quarter), 1.0, 0.0
    ).astype(jnp.bfloat16)
    split = jnp.dot(pick, merged, preferred_element_type=jnp.float32).astype(jnp.bfloat16)
    per_row = width // depth
    for t in range(n_tok):
        j, u = t // per_row, t % per_row
        cut[t] = split[j * quarter : (j + 1) * quarter, u * depth : (u + 1) * depth]

    def cut_copy(t, source):
        return send(
            cut.at[t], gathered.at[source, core], cut_send.at[t], cut_recv.at[source], {"tok": t}
        )

    def core_copy(t, c):
        return send(
            gathered.at[t, c], gathered.at[t, c], core_send.at[t], core_recv.at[t], sibling
        )

    def part_copy(t, source):
        return send(totals.at[t], parts.at[source], part_send.at[t], part_recv.at[source], {"tok": t})

    def pack_copy(t, source):
        return send(packed.at[t], arrived.at[source], pack_send.at[t], pack_recv.at[source], {"tok": t})

    for t in others:
        cut_copy(t, me).start()
    gathered[me, core] = cut[me]
    core_copy(me, core).start()
    for t in backward:
        cut_copy(t, t).wait_recv()
        core_copy(t, core).start()

    def meet(t):
        core_copy(t, 1 - core).wait_recv()
        block = gathered[t].reshape(2 * quarter, depth)
        return jnp.dot(block, merger_ref[...], preferred_element_type=jnp.float32).astype(jnp.bfloat16)

    for t in backward:
        text_copy(t, t).wait_recv()
        text_forward(t, grp).start()
    parts[me] = meet(me)
    for t in backward:
        totals[t] = meet(t)
        part_copy(t, me).start()
    total = parts[me].astype(jnp.float32)
    for t in others:
        part_copy(t, t).wait_recv()
        total = total + parts[t].astype(jnp.float32)
    sums = total.astype(jnp.bfloat16)
    capacity = packed.shape[1]
    slots = jnp.dot(slot_hit_ref[...], sums, preferred_element_type=jnp.float32).astype(jnp.bfloat16)
    packed[...] = slots.reshape(n_tok, capacity, slots.shape[1])
    for t in others:
        pack_copy(t, me).start()
    arrived[me] = packed[me]
    for t in backward:
        pack_copy(t, t).wait_recv()
    tokens = arrived[...].reshape(n_tok * capacity, arrived.shape[2])
    landed = jnp.dot(row_hit_ref[...], tokens, preferred_element_type=jnp.float32).astype(jnp.bfloat16)
    placed[...] = landed.reshape(placed.shape)
    last = send(placed.at[1 - core], out_ref.at[core], pair_sem.at[2], pair_sem.at[3], sibling)
    last.start()
    out_ref[core] = placed[core]
    last.wait()
    core_copy(me, core).wait_send()
    text_forward(me, grp).wait_send()
    text_forward(me, 1 - grp).wait_recv()
    for t in others:
        text_copy(t, me).wait_send()
        text_forward(t, grp).wait_send()
        text_forward(t, 1 - grp).wait_recv()
    for t in others:
        cut_copy(t, me).wait_send()
        core_copy(t, core).wait_send()
        part_copy(t, me).wait_send()
        pack_copy(t, me).wait_send()


def merged_tokens(heads, out_weight, patches, merger_weight, slot_hit, row_hit, text_blocks, n_tok):
    count, width = patches.shape
    depth, narrow = merger_weight.shape
    groups, capacity = count // 4, slot_hit.shape[0] // n_tok
    piece_rows = row_hit.shape[0]
    bf16 = jnp.bfloat16
    vmem = pl.BlockSpec(memory_space=pltpu.VMEM)
    each = pltpu.SemaphoreType.DMA((n_tok,))
    return pl.pallas_call(
        functools.partial(merge_kernel, n_tok),
        out_shape=(
            jax.ShapeDtypeStruct((2, piece_rows // 2, narrow), bf16),
            jax.ShapeDtypeStruct((2 * n_tok,) + text_blocks.shape[1:], bf16),
        ),
        in_specs=[vmem] * 7,
        out_specs=(vmem, vmem),
        scratch_shapes=[
            pltpu.VMEM((count // 2, width), bf16),
            pltpu.VMEM((count // 2, width), bf16),
            pltpu.VMEM((n_tok, groups // 2, depth), bf16),
            pltpu.VMEM((n_tok, 2, groups // 2, depth), bf16),
            pltpu.VMEM((n_tok, groups, narrow), bf16),
            pltpu.VMEM((n_tok, groups, narrow), bf16),
            pltpu.VMEM((n_tok, capacity, narrow), bf16),
            pltpu.VMEM((n_tok, capacity, narrow), bf16),
            pltpu.VMEM((2, piece_rows // 2, narrow), bf16),
            pltpu.SemaphoreType.DMA((4,)),
        ]
        + [each] * 9
        + [pltpu.SemaphoreType.DMA((2 * n_tok,)), each],
        compiler_params=pltpu.CompilerParams(
            collective_id=2, has_side_effects=True, vmem_limit_bytes=40 * 1024 * 1024
        ),
        cost_estimate=pl.CostEstimate(
            flops=2 * count * width * n_tok * LANES, bytes_accessed=8 * count * width, transcendentals=0
        ),
    )(heads, out_weight, patches, merger_weight, slot_hit, row_hit, text_blocks)


def shards(
    patches,
    image_sizes,
    vision_inproj,
    vision_outproj,
    merger_weight,
    text_embed,
    image_positions,
    prompt_lengths,
    decoder_inproj,
    decoder_outproj,
):
    n_tok = lax.axis_size("tok")
    half_width = vision_inproj.shape[3]
    head_local = half_width // HD
    if n_tok != head_local or lax.axis_size("sub") != 2 or lax.axis_size("grp") != 2:
        return shards_general(
            patches,
            image_sizes,
            vision_inproj,
            vision_outproj,
            merger_weight,
            text_embed,
            image_positions,
            prompt_lengths,
            decoder_inproj,
            decoder_outproj,
        )
    core = lax.axis_index("sub")
    patch_count, width = patches.shape
    piece_rows = text_embed.shape[0]
    bf16 = jnp.bfloat16

    vision_blocks = head_columns(vision_inproj, head_local)
    text_depth = decoder_inproj.shape[0]
    text_blocks = jnp.pad(head_columns(decoder_inproj, head_local), ((0, 0), (0, -text_depth % 16), (0, 0)))
    vision_out = lax.all_gather(turned(vision_outproj, head_local), "tok", axis=0, tiled=True)
    text_out = lax.all_gather(turned(decoder_outproj, head_local), ("grp", "tok"), axis=0, tiled=True)

    capacity = patch_count // (2 * n_tok)
    targets = image_positions[0]
    target_chip = targets // piece_rows
    target_row = targets % piece_rows
    chip_hits = (target_chip[:, None] == jnp.arange(n_tok, dtype=jnp.int32)[None, :]).astype(jnp.int32)
    slot_index = jnp.sum((jnp.cumsum(chip_hits, axis=0) - chip_hits) * chip_hits, axis=1)
    slot = target_chip * capacity + slot_index
    slot_hit = jnp.arange(n_tok * capacity, dtype=jnp.int32)[:, None] == slot[None, :]
    row_buffer = jnp.sum(jnp.where(slot_hit, target_row[None, :] + 1, 0), axis=1) - 1
    own_ends = jnp.broadcast_to(jnp.cumsum(image_sizes, axis=1), (n_tok, image_sizes.shape[1]))
    numbers = across(
        jnp.concatenate([row_buffer.reshape(n_tok, capacity), own_ends], axis=1), "tok"
    )
    arrived_rows, image_ends = numbers[:, :capacity].reshape(-1), numbers[:, capacity:]
    row_hit = jnp.arange(piece_rows, dtype=jnp.int32)[:, None] == arrived_rows[None, :]

    half_patches = lax.dynamic_slice_in_dim(patches, core * (patch_count // 2), patch_count // 2, 0)
    heads = heads_of("image", half_patches, vision_blocks, image_ends, n_tok)
    halves, text_parts = merged_tokens(
        heads,
        vision_out,
        patches,
        merger_weight,
        slot_hit.astype(bf16),
        row_hit.astype(bf16),
        text_blocks,
        n_tok,
    )
    text_weight = text_parts[:, :text_depth].reshape(width, 3 * LANES)
    half_piece = piece_rows // 2
    image_rows = halves.transpose(1, 0, 2).reshape(half_piece, width)
    filled = lax.dynamic_slice_in_dim(
        jnp.any(row_hit, axis=1).astype(jnp.int32), core * half_piece, half_piece, 0
    )
    text_half = lax.dynamic_slice_in_dim(text_embed, core * half_piece, half_piece, 0)
    decoder_input = jnp.where(filled[:, None] > 0, image_rows, text_half)

    starts = jnp.cumsum(prompt_lengths, axis=1) - prompt_lengths
    return heads_of("text", decoder_input, text_weight, starts, n_tok, text_out)


def solution(mesh):
    placed = (
        P(("grp", "tok"), None),
        P(("grp", "tok"), None),
        P("tok", "sub", None, None),
        P("sub", "tok"),
        P("tok", "sub"),
        P(("grp", "tok"), None),
        P("grp", "tok"),
        P("grp", None),
        P(("grp", "tok"), "sub", None, None),
        P("sub", ("grp", "tok")),
    )
    return jax.shard_map(
        shards,
        mesh=mesh,
        in_specs=placed,
        out_specs=P(("grp", "tok", "sub"), None),
        check_vma=False,
    )
```

```python
import functools
import math

import jax
import jax.numpy as jnp
from jax import lax
from jax.experimental import pallas as pl
from jax.experimental.pallas import tpu as pltpu
from jax.sharding import PartitionSpec as P

HD = 88
REACH = 3


norm_eps = 1e-06


def passed_along(block, axis, distance):
    devices = range(lax.axis_size(axis))
    route = [(i - distance, i) for i in devices if i - distance in devices]
    return lax.ppermute(block, axis, route)


def layer_norm(values):
    center = values - jnp.mean(values, axis=-1, keepdims=True)
    spread = jnp.mean(center * center, axis=-1, keepdims=True)
    return center * lax.rsqrt(spread + norm_eps)


def softmax_heads(queries, keys_all, values_all, allowed):
    scores = jnp.einsum("qhe,khe->hqk", queries, keys_all, preferred_element_type=jnp.float32) * (
        1.0 / math.sqrt(HD)
    )
    weights_raw = jnp.exp(scores) * allowed[None]
    weights = (weights_raw / jnp.sum(weights_raw, axis=-1, keepdims=True)).astype(jnp.bfloat16)
    mixture = jnp.einsum("hqk,khe->qhe", weights, values_all, preferred_element_type=jnp.float32)
    return mixture.astype(jnp.bfloat16)


def attend_blocks(queries, keys_all, values_all, allowed):
    row_total, head_count, head_size = queries.shape
    block_rows = min(row_total, 512)
    block_count = row_total // block_rows
    query_blocks = queries.reshape(block_count, block_rows, head_count, head_size)
    allow_blocks = allowed.reshape(block_count, block_rows, allowed.shape[1])
    outputs = lax.map(
        lambda block_pair: softmax_heads(block_pair[0], keys_all, values_all, block_pair[1]),
        (query_blocks, allow_blocks),
    )
    return outputs.reshape(row_total, head_count * head_size)


def shards_general(
    patches,
    image_sizes,
    vision_inproj,
    vision_outproj,
    merger_weight,
    text_embed,
    image_positions,
    prompt_lengths,
    decoder_inproj,
    decoder_outproj,
):
    inproj_full, outproj_full, merger_full = (
        lax.all_gather(vision_inproj, "tok", axis=0, tiled=True),
        lax.all_gather(vision_outproj, "tok", axis=1, tiled=True),
        lax.all_gather(merger_weight, "tok", axis=0, tiled=True),
    )
    patch_count, width = patches.shape
    half_width = inproj_full.shape[3]
    head_local = half_width // HD
    patch_rows = patches.astype(jnp.float32)
    normed = layer_norm(patch_rows).astype(jnp.bfloat16)
    projected = jnp.dot(
        normed, inproj_full.reshape(width, 3 * half_width), preferred_element_type=jnp.float32
    )
    triple = projected.astype(jnp.bfloat16).reshape(patch_count, 3, head_local, HD)
    image_ends = jnp.cumsum(image_sizes[0])
    group_ids = jnp.arange(patch_count, dtype=jnp.int32) // 4
    image_ids = jnp.sum((group_ids[:, None] >= image_ends[None, :]).astype(jnp.int32), axis=1)
    same_image = (image_ids[:, None] == image_ids[None, :]).astype(jnp.float32)
    heads_out = attend_blocks(triple[:, 0], triple[:, 1], triple[:, 2], same_image)
    partial_value = jnp.dot(heads_out, outproj_full, preferred_element_type=jnp.float32)
    hidden = patch_rows + lax.psum(partial_value.astype(jnp.bfloat16), "sub").astype(jnp.float32)
    merged = layer_norm(hidden).astype(jnp.bfloat16).reshape(patch_count // 4, 4 * width)
    piece_count = lax.axis_size("tok")
    capacity = patch_count // (2 * piece_count)
    piece_rows = text_embed.shape[0]
    targets = image_positions[0]
    target_chip = targets // piece_rows
    target_row = targets % piece_rows
    chip_hits = (target_chip[:, None] == jnp.arange(piece_count, dtype=jnp.int32)[None, :]).astype(
        jnp.int32
    )
    slot_index = jnp.sum((jnp.cumsum(chip_hits, axis=0) - chip_hits) * chip_hits, axis=1)
    row_buffer = (
        jnp.full((piece_count, capacity), piece_rows, jnp.int32)
        .at[target_chip, slot_index]
        .set(target_row)
    )
    embedded = jnp.dot(merged, merger_full, preferred_element_type=jnp.float32).astype(jnp.bfloat16)
    narrow_rows = lax.all_to_all(
        jnp.zeros((piece_count, capacity, embedded.shape[1]), embedded.dtype)
        .at[target_chip, slot_index]
        .set(embedded),
        "tok",
        split_axis=0,
        concat_axis=0,
        tiled=True,
    )
    arrived_rows = lax.all_to_all(row_buffer, "tok", split_axis=0, concat_axis=0, tiled=True)
    image_half = narrow_rows.reshape(piece_count * capacity, half_width)
    image_full = lax.all_gather(image_half, "sub", axis=1, tiled=True)
    decoder_input = text_embed.at[arrived_rows.reshape(-1)].set(image_full, mode="drop")
    text_inproj, text_outproj = (
        lax.all_gather(decoder_inproj, ("grp", "tok"), axis=0, tiled=True),
        lax.all_gather(decoder_outproj, ("grp", "tok"), axis=1, tiled=True),
    )
    normed_text = layer_norm(decoder_input.astype(jnp.float32)).astype(jnp.bfloat16)
    text_proj = jnp.dot(
        normed_text, text_inproj.reshape(width, 3 * half_width), preferred_element_type=jnp.float32
    )
    text_triple = text_proj.astype(jnp.bfloat16).reshape(piece_rows, 3, head_local, HD)
    own_pair = text_triple[:, 1:].reshape(piece_rows, 2 * half_width)
    earlier = [own_pair]
    carried = own_pair
    for step_back in range(REACH):
        carried = passed_along(carried, "tok", 1)
        earlier.append(carried)
    window = jnp.concatenate(earlier[::-1], axis=0).reshape(
        (REACH + 1) * piece_rows, 2, head_local, HD
    )
    piece_id = lax.axis_index("tok")
    query_pos = piece_id * piece_rows + jnp.arange(piece_rows, dtype=jnp.int32)
    key_pos = (piece_id - REACH) * piece_rows + jnp.arange(
        (REACH + 1) * piece_rows, dtype=jnp.int32
    )
    lengths = prompt_lengths[0]
    starts = jnp.cumsum(lengths) - lengths
    query_start = jnp.max(
        jnp.where(starts[None, :] <= query_pos[:, None], starts[None, :], 0), axis=1
    )
    allowed = (
        (key_pos[None, :] <= query_pos[:, None]) & (key_pos[None, :] >= query_start[:, None])
    ).astype(jnp.float32)
    text_heads = attend_blocks(text_triple[:, 0], window[:, 0], window[:, 1], allowed)
    text_partial = jnp.dot(text_heads, text_outproj, preferred_element_type=jnp.float32)
    return lax.psum_scatter(
        text_partial.astype(jnp.bfloat16), "sub", scatter_dimension=0, tiled=True
    )


LANES = 128
MESH = pl.DeviceIdType.MESH


def head_kernel(
    kind,
    n_tok,
    x_ref,
    weight_ref,
    info_ref,
    *rest,
):
    if kind == "image":
        out_ref, buf, staged, kv, send_sem, recv_sem, back_send, back_recv, *own_scratch = rest
        w_ref, w_send, w_recv, w_pass = own_scratch
        mixed = out_ref
    else:
        last_weight_ref, out_ref, buf, staged, kv, send_sem, recv_sem, back_send, back_recv, *own_scratch = rest
        mixed, give, got, pair_sem = own_scratch
        w_ref = weight_ref
    me, core, grp = lax.axis_index("tok"), lax.axis_index("sub"), lax.axis_index("grp")
    rows = 2 * x_ref.shape[0]
    z, y = lax.div(me, 2), lax.rem(me, 2)
    n_z = n_tok // 2
    side = me + 1 - 2 * y

    barrier = pltpu.get_barrier_semaphore()
    for d in range(1, n_tok):
        pl.semaphore_signal(
            barrier, inc=1, device_id={"tok": lax.rem(me + d, n_tok)}, device_id_type=MESH
        )
    pl.semaphore_signal(barrier, inc=1, device_id={"sub": 1 - core}, device_id_type=MESH)

    greeted = n_tok
    if kind == "image":
        pl.semaphore_signal(barrier, inc=1, device_id={"grp": 1 - grp}, device_id_type=MESH)
        greeted = n_tok + 1
        w_ref[me] = weight_ref[me]
    own = x_ref[...].astype(jnp.float32)
    buf[me, core] = layer_norm(own).astype(jnp.bfloat16)
    pl.semaphore_wait(barrier, greeted)

    def push(t, way):
        target = [{"tok": me + 2}, {"tok": me - 2}, {"tok": side}, {"sub": 1 - core}][way]
        return pltpu.make_async_remote_copy(
            src_ref=buf.at[t, core],
            dst_ref=buf.at[t, core],
            send_sem=send_sem.at[way, t],
            recv_sem=recv_sem.at[t, core],
            device_id=target,
            device_id_type=MESH,
        )

    def arrived(t, c):
        pltpu.make_async_remote_copy(
            src_ref=buf.at[t, c],
            dst_ref=buf.at[t, c],
            send_sem=send_sem.at[3, t],
            recv_sem=recv_sem.at[t, c],
            device_id={"sub": 1 - core},
            device_id_type=MESH,
        ).wait_recv()

    def run(act, wait, between=lambda: None):
        @pl.when(z < n_z - 1)
        def _():
            act(me, 0)

        @pl.when(z > 0)
        def _():
            act(me, 1)

        act(me, 2)
        act(me, 3)
        for k in range(1, n_z + 1):
            if k < n_z:
                @pl.when(z - k >= 0)
                def _():
                    wait(me - 2 * k)

                    @pl.when(z < n_z - 1)
                    def _():
                        act(me - 2 * k, 0)

                    act(me - 2 * k, 2)
                    act(me - 2 * k, 3)

                @pl.when(z + k < n_z)
                def _():
                    wait(me + 2 * k)

                    @pl.when(z > 0)
                    def _():
                        act(me + 2 * k, 1)

                    act(me + 2 * k, 2)
                    act(me + 2 * k, 3)

            if k == 2:
                between()
            if k == 1:
                wait(side)
                act(side, 3)
            else:
                @pl.when(z - k + 1 >= 0)
                def _():
                    wait(side - 2 * k + 2)
                    act(side - 2 * k + 2, 3)

                @pl.when(z + k - 1 < n_z)
                def _():
                    wait(side + 2 * k - 2)
                    act(side + 2 * k - 2, 3)

    def weight_copy(t, source):
        return pltpu.make_async_remote_copy(
            src_ref=weight_ref.at[t],
            dst_ref=w_ref.at[source],
            send_sem=w_send.at[t],
            recv_sem=w_recv.at[source],
            device_id={"tok": t},
            device_id_type=MESH,
        )

    def weight_pass(t):
        return pltpu.make_async_remote_copy(
            src_ref=w_ref.at[t],
            dst_ref=w_ref.at[t],
            send_sem=w_pass.at[t],
            recv_sem=w_recv.at[t],
            device_id={"grp": 1 - grp},
            device_id_type=MESH,
        )

    others = [lax.rem(me + d, n_tok) for d in range(1, n_tok)]

    def mine(t):
        return lax.rem(lax.div(t, 2), 2) == grp

    if kind == "image":
        @pl.when(mine(me))
        def _():
            for t in others:
                weight_copy(t, me).start()

    def hand_over():
        for t in others:
            @pl.when(mine(t))
            def _():
                weight_copy(t, t).wait_recv()
                weight_pass(t).start()

    if kind == "image":
        run(lambda t, way: push(t, way).start(), lambda t: arrived(t, core), hand_over)
        for t in others:
            @pl.when(jnp.logical_not(mine(t)))
            def _():
                weight_pass(t).wait_recv()
    else:
        run(lambda t, way: push(t, way).start(), lambda t: arrived(t, core))

    for t in range(n_tok):
        arrived(t, 1 - core)

    def project(j):
        block = buf[j].reshape(rows, buf.shape[3])
        weight = w_ref[...].reshape(buf.shape[3], 3 * LANES)
        return jnp.dot(block, weight, preferred_element_type=jnp.float32).astype(jnp.bfloat16)

    def mix(query, key, value, allowed):
        scores = lax.dot_general(
            query, key, (((1,), (1,)), ((), ())), preferred_element_type=jnp.float32
        ) * (1.0 / math.sqrt(HD))
        raw = jnp.where(allowed, jnp.exp(scores), 0.0)
        weights = (raw / jnp.sum(raw, axis=-1, keepdims=True)).astype(jnp.bfloat16)
        return jnp.dot(weights, value, preferred_element_type=jnp.float32).astype(jnp.bfloat16)

    def back(j):
        return pltpu.make_async_remote_copy(
            src_ref=staged.at[j],
            dst_ref=mixed.at[me],
            send_sem=back_send.at[j],
            recv_sem=back_recv.at[me],
            device_id={"tok": j},
            device_id_type=MESH,
        )

    if kind == "text":
        kv[pl.ds(0, REACH)] = jnp.zeros((REACH, rows, 3 * LANES), jnp.bfloat16)

        def fill(j, carry):
            kv[j + REACH] = project(j)
            return carry

        lax.fori_loop(0, n_tok, fill, 0)

    def piece(d, carry):
        j = lax.rem(me + d, n_tok)
        if kind == "image":
            proj = project(j)
            query, key, value = (proj[:, i * LANES : (i + 1) * LANES] for i in range(3))
            left = lax.div(lax.broadcasted_iota(jnp.int32, (rows, 1), 0), 4)
            right = lax.div(lax.broadcasted_iota(jnp.int32, (1, rows), 1), 4)
            left_id, right_id = jnp.zeros_like(left), jnp.zeros_like(right)
            for i in range(info_ref.shape[1]):
                end = info_ref[j, i]
                left_id = left_id + jnp.where(left >= end, 1, 0)
                right_id = right_id + jnp.where(right >= end, 1, 0)
            allowed = left_id == right_id
        else:
            span = (REACH + 1) * rows
            query = kv[j + REACH, :, 0:LANES]
            key = kv[pl.ds(j, REACH + 1), :, LANES : 2 * LANES].reshape(span, LANES)
            value = kv[pl.ds(j, REACH + 1), :, 2 * LANES : 3 * LANES].reshape(span, LANES)
            query_pos = j * rows + lax.broadcasted_iota(jnp.int32, (rows, 1), 0)
            key_pos = (j - REACH) * rows + lax.broadcasted_iota(jnp.int32, (1, span), 1)
            begin = jnp.zeros_like(query_pos)
            for i in range(info_ref.shape[1]):
                first = info_ref[0, i]
                begin = jnp.maximum(begin, jnp.where(query_pos >= first, first, 0))
            allowed = (key_pos <= query_pos) & (key_pos >= begin)
        mixture = mix(query, key, value, allowed)

        @pl.when(d < n_tok)
        def _():
            staged[j] = mixture
            back(j).start()

        @pl.when(d == n_tok)
        def _():
            mixed[me] = mixture

        return carry

    lax.fori_loop(1, n_tok + 1, piece, 0)

    run(lambda t, way: push(t, way).wait_send(), lambda t: None)
    for d in range(1, n_tok):
        j = lax.rem(me + d, n_tok)
        back(j).wait_send()
        pltpu.make_async_remote_copy(
            src_ref=staged.at[j],
            dst_ref=mixed.at[j],
            send_sem=back_send.at[j],
            recv_sem=back_recv.at[j],
            device_id={"tok": j},
            device_id_type=MESH,
        ).wait_recv()
    if kind == "image":
        @pl.when(mine(me))
        def _():
            for t in others:
                weight_copy(t, me).wait_send()

        for t in others:
            @pl.when(mine(t))
            def _():
                weight_pass(t).wait_send()

        return

    half = rows // 2

    def projected(c):
        total = jnp.zeros((half, out_ref.shape[1]), jnp.float32)
        for h in range(n_tok):
            total = total + lax.dot_general(
                mixed[h, pl.ds(pl.multiple_of(c * half, half), half), 0:HD],
                last_weight_ref[:, h * HD : (h + 1) * HD],
                (((1,), (1,)), ((), ())),
                preferred_element_type=jnp.float32,
            )
        return total.astype(jnp.bfloat16)

    give[...] = projected(1 - core)
    swap = pltpu.make_async_remote_copy(
        src_ref=give,
        dst_ref=got,
        send_sem=pair_sem.at[0],
        recv_sem=pair_sem.at[1],
        device_id={"sub": 1 - core},
        device_id_type=MESH,
    )
    swap.start()
    kept = projected(core)
    swap.wait()
    out_ref[...] = (kept.astype(jnp.float32) + got[...].astype(jnp.float32)).astype(jnp.bfloat16)


def heads_of(kind, half_rows, weight, info, n_tok, last_weight=None):
    half, width = half_rows.shape
    rows = 2 * half
    bf16 = jnp.bfloat16
    vmem = pl.BlockSpec(memory_space=pltpu.VMEM)
    total = n_tok * rows
    each = pltpu.SemaphoreType.DMA((n_tok,))
    mixed = (n_tok, rows, LANES)
    operands = [half_rows, weight, info]
    if kind == "image":
        out_shape, kv_shape = mixed, (1, 16, LANES)
        extra = [pltpu.VMEM(weight.shape, bf16), each, each, each]
    else:
        out_shape, kv_shape = (half, width), (n_tok + REACH, rows, 3 * LANES)
        operands.append(last_weight)
        extra = [
            pltpu.VMEM(mixed, bf16),
            pltpu.VMEM((half, width), bf16),
            pltpu.VMEM((half, width), bf16),
            pltpu.SemaphoreType.DMA((2,)),
        ]
    return pl.pallas_call(
        functools.partial(head_kernel, kind, n_tok),
        out_shape=jax.ShapeDtypeStruct(out_shape, bf16),
        in_specs=[vmem, vmem, pl.BlockSpec(memory_space=pltpu.SMEM)] + [vmem] * (len(operands) - 3),
        out_specs=vmem,
        scratch_shapes=[
            pltpu.VMEM((n_tok, 2, half, width), bf16),
            pltpu.VMEM(mixed, bf16),
            pltpu.VMEM(kv_shape, bf16),
            pltpu.SemaphoreType.DMA((4, n_tok)),
            pltpu.SemaphoreType.DMA((n_tok, 2)),
            each,
            each,
        ]
        + extra,
        compiler_params=pltpu.CompilerParams(
            collective_id=0 if kind == "image" else 1,
            has_side_effects=True,
            vmem_limit_bytes=40 * 1024 * 1024,
        ),
        cost_estimate=pl.CostEstimate(
            flops=2 * total * width * 3 * LANES, bytes_accessed=2 * total * width, transcendentals=0
        ),
    )(*operands)


def head_columns(weight, head_local):
    rows = weight.shape[0]
    split = weight.reshape(rows, 3, head_local, HD).transpose(2, 0, 1, 3)
    split = jnp.pad(split, ((0, 0), (0, 0), (0, 0), (0, LANES - HD)))
    return split.reshape(head_local, rows, 3 * LANES)


def across(block, axis):
    return lax.all_to_all(block, axis, split_axis=0, concat_axis=0, tiled=True)


def merge_kernel(
    n_tok,
    heads_ref,
    out_weight_ref,
    patches_ref,
    merger_ref,
    slot_hit_ref,
    row_hit_ref,
    text_weight_ref,
    out_ref,
    text_out_ref,
    give,
    got,
    cut,
    gathered,
    totals,
    parts,
    packed,
    arrived,
    placed,
    pair_sem,
    cut_send,
    cut_recv,
    core_send,
    core_recv,
    part_send,
    part_recv,
    pack_send,
    pack_recv,
    text_send,
    text_recv,
    text_pass,
):
    me, core, grp = lax.axis_index("tok"), lax.axis_index("sub"), lax.axis_index("grp")
    half, width = give.shape
    quarter = half // 4
    depth = merger_ref.shape[0]

    barrier = pltpu.get_barrier_semaphore()
    for d in range(1, n_tok):
        pl.semaphore_signal(
            barrier, inc=1, device_id={"tok": lax.rem(me + d, n_tok)}, device_id_type=MESH
        )
    pl.semaphore_signal(barrier, inc=1, device_id={"sub": 1 - core}, device_id_type=MESH)
    pl.semaphore_signal(barrier, inc=1, device_id={"grp": 1 - grp}, device_id_type=MESH)

    def send(src, dst, send_sem, recv_sem, target):
        return pltpu.make_async_remote_copy(
            src_ref=src,
            dst_ref=dst,
            send_sem=send_sem,
            recv_sem=recv_sem,
            device_id=target,
            device_id_type=MESH,
        )

    def projected(c):
        total = jnp.zeros((half, width), jnp.float32)
        for h in range(n_tok):
            total = total + lax.dot_general(
                heads_ref[h, pl.ds(pl.multiple_of(c * half, half), half), 0:HD],
                out_weight_ref[:, h * HD : (h + 1) * HD],
                (((1,), (1,)), ((), ())),
                preferred_element_type=jnp.float32,
            )
        return total.astype(jnp.bfloat16)

    sibling = {"sub": 1 - core}
    def text_copy(t, source):
        return send(
            text_weight_ref.at[t],
            text_out_ref.at[grp * n_tok + source],
            text_send.at[t],
            text_recv.at[grp * n_tok + source],
            {"tok": t},
        )

    def text_forward(t, g):
        slot = g * n_tok + t
        return send(
            text_out_ref.at[slot],
            text_out_ref.at[slot],
            text_pass.at[t],
            text_recv.at[slot],
            {"grp": 1 - grp},
        )

    others = [lax.rem(me + d, n_tok) for d in range(1, n_tok)]
    backward = [lax.rem(me + n_tok - d, n_tok) for d in range(1, n_tok)]
    text_out_ref[grp * n_tok + me] = text_weight_ref[me]
    pl.semaphore_wait(barrier, n_tok + 1)
    for t in others:
        text_copy(t, me).start()
    text_forward(me, grp).start()
    give[...] = projected(1 - core)
    swap = send(give, got, pair_sem.at[0], pair_sem.at[1], sibling)
    swap.start()
    kept = projected(core)
    swap.wait()
    rows = patches_ref[pl.ds(pl.multiple_of(core * half, half), half)].astype(jnp.float32)
    hidden = rows + (kept.astype(jnp.float32) + got[...].astype(jnp.float32))
    merged = layer_norm(hidden).astype(jnp.bfloat16)
    to_row = lax.broadcasted_iota(jnp.int32, (half, half), 0)
    from_row = lax.broadcasted_iota(jnp.int32, (half, half), 1)
    pick = jnp.where(
        from_row == 4 * lax.rem(to_row, quarter) + lax.div(to_row, quarter), 1.0, 0.0
    ).astype(jnp.bfloat16)
    split = jnp.dot(pick, merged, preferred_element_type=jnp.float32).astype(jnp.bfloat16)
    per_row = width // depth
    for t in range(n_tok):
        j, u = t // per_row, t % per_row
        cut[t] = split[j * quarter : (j + 1) * quarter, u * depth : (u + 1) * depth]

    def cut_copy(t, source):
        return send(
            cut.at[t], gathered.at[source, core], cut_send.at[t], cut_recv.at[source], {"tok": t}
        )

    def core_copy(t, c):
        return send(
            gathered.at[t, c], gathered.at[t, c], core_send.at[t], core_recv.at[t], sibling
        )

    def part_copy(t, source):
        return send(totals.at[t], parts.at[source], part_send.at[t], part_recv.at[source], {"tok": t})

    def pack_copy(t, source):
        return send(packed.at[t], arrived.at[source], pack_send.at[t], pack_recv.at[source], {"tok": t})

    for t in others:
        cut_copy(t, me).start()
    gathered[me, core] = cut[me]
    core_copy(me, core).start()
    for t in backward:
        cut_copy(t, t).wait_recv()
        core_copy(t, core).start()

    def meet(t):
        core_copy(t, 1 - core).wait_recv()
        block = gathered[t].reshape(2 * quarter, depth)
        return jnp.dot(block, merger_ref[...], preferred_element_type=jnp.float32).astype(jnp.bfloat16)

    for t in backward:
        text_copy(t, t).wait_recv()
        text_forward(t, grp).start()
    parts[me] = meet(me)
    for t in backward:
        totals[t] = meet(t)
        part_copy(t, me).start()
    total = parts[me].astype(jnp.float32)
    for t in others:
        part_copy(t, t).wait_recv()
        total = total + parts[t].astype(jnp.float32)
    sums = total.astype(jnp.bfloat16)
    capacity = packed.shape[1]
    slots = jnp.dot(slot_hit_ref[...], sums, preferred_element_type=jnp.float32).astype(jnp.bfloat16)
    packed[...] = slots.reshape(n_tok, capacity, slots.shape[1])
    for t in others:
        pack_copy(t, me).start()
    arrived[me] = packed[me]
    for t in backward:
        pack_copy(t, t).wait_recv()
    tokens = arrived[...].reshape(n_tok * capacity, arrived.shape[2])
    landed = jnp.dot(row_hit_ref[...], tokens, preferred_element_type=jnp.float32).astype(jnp.bfloat16)
    placed[...] = landed.reshape(placed.shape)
    last = send(placed.at[1 - core], out_ref.at[core], pair_sem.at[2], pair_sem.at[3], sibling)
    last.start()
    out_ref[core] = placed[core]
    last.wait()
    core_copy(me, core).wait_send()
    text_forward(me, grp).wait_send()
    text_forward(me, 1 - grp).wait_recv()
    for t in others:
        text_copy(t, me).wait_send()
        text_forward(t, grp).wait_send()
        text_forward(t, 1 - grp).wait_recv()
    for t in others:
        cut_copy(t, me).wait_send()
        core_copy(t, core).wait_send()
        part_copy(t, me).wait_send()
        pack_copy(t, me).wait_send()


def merged_tokens(heads, out_weight, patches, merger_weight, slot_hit, row_hit, text_blocks, n_tok):
    count, width = patches.shape
    depth, narrow = merger_weight.shape
    groups, capacity = count // 4, slot_hit.shape[0] // n_tok
    piece_rows = row_hit.shape[0]
    bf16 = jnp.bfloat16
    vmem = pl.BlockSpec(memory_space=pltpu.VMEM)
    each = pltpu.SemaphoreType.DMA((n_tok,))
    return pl.pallas_call(
        functools.partial(merge_kernel, n_tok),
        out_shape=(
            jax.ShapeDtypeStruct((2, piece_rows // 2, narrow), bf16),
            jax.ShapeDtypeStruct((2 * n_tok,) + text_blocks.shape[1:], bf16),
        ),
        in_specs=[vmem] * 7,
        out_specs=(vmem, vmem),
        scratch_shapes=[
            pltpu.VMEM((count // 2, width), bf16),
            pltpu.VMEM((count // 2, width), bf16),
            pltpu.VMEM((n_tok, groups // 2, depth), bf16),
            pltpu.VMEM((n_tok, 2, groups // 2, depth), bf16),
            pltpu.VMEM((n_tok, groups, narrow), bf16),
            pltpu.VMEM((n_tok, groups, narrow), bf16),
            pltpu.VMEM((n_tok, capacity, narrow), bf16),
            pltpu.VMEM((n_tok, capacity, narrow), bf16),
            pltpu.VMEM((2, piece_rows // 2, narrow), bf16),
            pltpu.SemaphoreType.DMA((4,)),
        ]
        + [each] * 9
        + [pltpu.SemaphoreType.DMA((2 * n_tok,)), each],
        compiler_params=pltpu.CompilerParams(
            collective_id=2, has_side_effects=True, vmem_limit_bytes=40 * 1024 * 1024
        ),
        cost_estimate=pl.CostEstimate(
            flops=2 * count * width * n_tok * LANES, bytes_accessed=8 * count * width, transcendentals=0
        ),
    )(heads, out_weight, patches, merger_weight, slot_hit, row_hit, text_blocks)


def shards(
    patches,
    image_sizes,
    vision_inproj,
    vision_outproj,
    merger_weight,
    text_embed,
    image_positions,
    prompt_lengths,
    decoder_inproj,
    decoder_outproj,
):
    n_tok = lax.axis_size("tok")
    half_width = vision_inproj.shape[3]
    head_local = half_width // HD
    if n_tok != head_local or lax.axis_size("sub") != 2 or lax.axis_size("grp") != 2:
        return shards_general(
            patches,
            image_sizes,
            vision_inproj,
            vision_outproj,
            merger_weight,
            text_embed,
            image_positions,
            prompt_lengths,
            decoder_inproj,
            decoder_outproj,
        )
    core = lax.axis_index("sub")
    patch_count, width = patches.shape
    piece_rows = text_embed.shape[0]
    bf16 = jnp.bfloat16

    vision_blocks = head_columns(vision_inproj, head_local)
    text_depth = decoder_inproj.shape[0]
    text_blocks = jnp.pad(head_columns(decoder_inproj, head_local), ((0, 0), (0, -text_depth % 16), (0, 0)))
    vision_out = lax.all_gather(vision_outproj.T, "tok", axis=0, tiled=True)
    text_out = lax.all_gather(decoder_outproj.T, ("grp", "tok"), axis=0, tiled=True)

    capacity = patch_count // (2 * n_tok)
    targets = image_positions[0]
    target_chip = targets // piece_rows
    target_row = targets % piece_rows
    chip_hits = (target_chip[:, None] == jnp.arange(n_tok, dtype=jnp.int32)[None, :]).astype(jnp.int32)
    slot_index = jnp.sum((jnp.cumsum(chip_hits, axis=0) - chip_hits) * chip_hits, axis=1)
    slot = target_chip * capacity + slot_index
    slot_hit = jnp.arange(n_tok * capacity, dtype=jnp.int32)[:, None] == slot[None, :]
    row_buffer = jnp.sum(jnp.where(slot_hit, target_row[None, :] + 1, 0), axis=1) - 1
    own_ends = jnp.broadcast_to(jnp.cumsum(image_sizes, axis=1), (n_tok, image_sizes.shape[1]))
    numbers = across(
        jnp.concatenate([row_buffer.reshape(n_tok, capacity), own_ends], axis=1), "tok"
    )
    arrived_rows, image_ends = numbers[:, :capacity].reshape(-1), numbers[:, capacity:]
    row_hit = jnp.arange(piece_rows, dtype=jnp.int32)[:, None] == arrived_rows[None, :]

    half_patches = lax.dynamic_slice_in_dim(patches, core * (patch_count // 2), patch_count // 2, 0)
    heads = heads_of("image", half_patches, vision_blocks, image_ends, n_tok)
    halves, text_parts = merged_tokens(
        heads,
        vision_out,
        patches,
        merger_weight,
        slot_hit.astype(bf16),
        row_hit.astype(bf16),
        text_blocks,
        n_tok,
    )
    text_weight = text_parts[:, :text_depth].reshape(width, 3 * LANES)
    half_piece = piece_rows // 2
    image_rows = halves.transpose(1, 0, 2).reshape(half_piece, width)
    filled = lax.dynamic_slice_in_dim(
        jnp.any(row_hit, axis=1).astype(jnp.int32), core * half_piece, half_piece, 0
    )
    text_half = lax.dynamic_slice_in_dim(text_embed, core * half_piece, half_piece, 0)
    decoder_input = jnp.where(filled[:, None] > 0, image_rows, text_half)

    starts = jnp.cumsum(prompt_lengths, axis=1) - prompt_lengths
    return heads_of("text", decoder_input, text_weight, starts, n_tok, text_out)


def solution(mesh):
    placed = (
        P(("grp", "tok"), None),
        P(("grp", "tok"), None),
        P("tok", "sub", None, None),
        P("sub", "tok"),
        P("tok", "sub"),
        P(("grp", "tok"), None),
        P("grp", "tok"),
        P("grp", None),
        P(("grp", "tok"), "sub", None, None),
        P("sub", ("grp", "tok")),
    )
    return jax.shard_map(
        shards,
        mesh=mesh,
        in_specs=placed,
        out_specs=P(("grp", "tok", "sub"), None),
        check_vma=False,
    )
```
